512 devices in a mesh: row: 32 (over z_lo, y), col: 16 (over x, z_hi, core).
Axes of the slice: x: 4, y: 4, z: 16 (z_hi: 2, z_lo: 8; z = z_hi * 8 + z_lo), core: 2. Of those that a mesh axis runs over, the one named last changes fastest.
Arguments:
- covariance: float32 [12288, 12288], P('row', 'col'), as said below
- rotations: float32 [2, 16, 768, 768], P(None, 'col', 'row')
- flips: int32 [2, 16], replicated, may hold values 0 or 1
Outputs:
- rotated: float32 [12288, 12288], P('row', 'col')
The draws below stay inside these ranges and needn't reach their ends.
Inputs may be any that keep to these rules, and one draw needn't show every extreme that they name: covariance is exactly symmetric.
All inputs are finite; a program needn't handle non-finite values.
Results may differ from the reference program's by a relative error of at most 0.00019.
Values sent between devices are 32-bit elements; how exact they have to be, the bound alone decides.
A program may use at most 64 MiB of HBM per device.

```python
import jax
import jax.numpy as jnp
from jax import lax

BLOCK_ORDER = 384
ROUNDS = 2
PAIR_COUNT = 16
BLOCK_COUNT = 32
PAIR_ORDER = 768
MATRIX_ORDER = 12288


def draw_covariance(key, part):
    key = jax.random.fold_in(key, 11)
    first, second = jax.random.split(key)
    noise = jax.random.normal(first, (MATRIX_ORDER, MATRIX_ORDER), jnp.float32)
    scales = jnp.exp(jax.random.uniform(second, (MATRIX_ORDER,), jnp.float32, jnp.log(0.4), jnp.log(2.5)))
    outer = scales[:, None] * scales[None, :]
    index = jnp.arange(MATRIX_ORDER)
    diagonal = jnp.where(index[:, None] == index[None, :], 2.0, 0.0)
    return (0.5 * (noise + noise.T) + diagonal) * outer


def draw_rotations(key, part):
    key = jax.random.fold_in(key, 23)
    shape = (ROUNDS, PAIR_COUNT, PAIR_ORDER, PAIR_ORDER)
    noise = jax.random.normal(key, shape, jnp.float32)
    index = jnp.arange(PAIR_ORDER)
    identity = jnp.where(index[:, None] == index[None, :], 1.0, 0.0)
    return identity + noise * (0.5 / PAIR_ORDER ** 0.5)


def set_ends(result, key, low, top_value):
    dims = result.shape
    index_at = [jax.random.randint(jax.random.fold_in(key, axis), (), 0, dims[axis]) for axis in range(len(dims))]
    result = result.at[tuple(index_at)].set(low)
    longest = dims.index(max(dims))
    index_at[longest] = (index_at[longest] + 1) % dims[longest]
    return result.at[tuple(index_at)].set(top_value)


def setup_inputs(seed: int = 0) -> dict:
    key_list = jax.random.split(jax.random.key(seed), 4)
    covariance = draw_covariance(jax.random.fold_in(key_list[3], 71), 0)
    rotations = draw_rotations(jax.random.fold_in(key_list[3], 71), 0)
    flips = set_ends((jax.random.randint(key_list[2], (ROUNDS, PAIR_COUNT), 0, 2) < 1).astype(jnp.int32), jax.random.fold_in(key_list[2], 1), 0, 1)
    return dict(covariance=covariance, rotations=rotations, flips=flips)


def tournament_source():
    position = jnp.arange(BLOCK_COUNT, dtype=jnp.int32)
    pair_of = position // 2
    even_source = jnp.where(pair_of == 0, 0, jnp.where(pair_of == 1, 1, 2 * (pair_of - 1)))
    odd_source = jnp.where(pair_of < PAIR_COUNT - 1, 2 * (pair_of + 1) + 1, 2 * (PAIR_COUNT - 1))
    return jnp.where(position % 2 == 0, even_source, odd_source).astype(jnp.int32)


def reference(covariance, rotations, flips):
    matrix = covariance
    position = jnp.arange(BLOCK_COUNT, dtype=jnp.int32)
    moving = tournament_source()
    for step in range(ROUNDS):
        turn = rotations[step]
        columns = matrix.reshape(MATRIX_ORDER, PAIR_COUNT, PAIR_ORDER)
        right = jnp.einsum("xpa,pab->xpb", columns, turn, precision=lax.Precision.HIGHEST)
        rows_view = right.reshape(PAIR_COUNT, PAIR_ORDER, MATRIX_ORDER)
        left = jnp.einsum("pax,pab->pbx", rows_view, turn, precision=lax.Precision.HIGHEST)
        matrix = left.reshape(MATRIX_ORDER, MATRIX_ORDER)
        source = jnp.bitwise_xor(position, flips[step][position // 2]).astype(jnp.int32)
        if step + 1 < ROUNDS:
            source = source[moving]
        blocks = matrix.reshape(BLOCK_COUNT, BLOCK_ORDER, BLOCK_COUNT, BLOCK_ORDER)
        blocks = jnp.take(blocks, source, axis=0)
        blocks = jnp.take(blocks, source, axis=2)
        matrix = blocks.reshape(MATRIX_ORDER, MATRIX_ORDER)
    return matrix
```

```python
import functools

import jax
import jax.numpy as jnp
from jax import lax
from jax.experimental import pallas as pl
from jax.experimental.pallas import tpu as pltpu
from jax.sharding import PartitionSpec as P

ROUNDS = 2
ORDER = 384
PAIR = 768
LAYERS = 8
SIDES = 4
PIECE = 24
MESH = pl.DeviceIdType.MESH


def split(value):
    high = value.astype(jnp.bfloat16)
    return high, (value - high.astype(jnp.float32)).astype(jnp.bfloat16)


def product(first, second):
    one = functools.partial(jnp.dot, preferred_element_type=jnp.float32)
    return one(first[0], second[0]) + (one(first[0], second[1]) + one(first[1], second[0]))


def moved_to(place):
    even = jnp.where(place == 0, 0, jnp.where(place == 30, 31, place + 2))
    return jnp.where(place % 2 == 0, even, jnp.where(place == 1, 2, place - 2))


def came_from(place):
    even = jnp.where(place == 0, 0, jnp.where(place == 2, 1, place - 2))
    return jnp.where(place % 2 == 0, even, jnp.where(place == 31, 30, place + 2))


def crosses(place):
    edge = place % 4
    return ((edge == 0) & (place != 0)) | ((edge == 3) & (place != 31))


def kernel(
    tile, turn, out, right, left, other, fresh, block, flipped, left_high, left_low, mid_high,
    mid_low, own_sem, other_sem, right_sem, left_sem, spread_sem, fresh_sem, chain_out, side_out,
    relay_out, left_out, spread_out, other_out, block_out, flipped_out, pass_out,
):
    row, col = lax.axis_index("row"), lax.axis_index("col")
    layer, side = row // SIDES, row % SIDES
    along, far, core = col // 4, (col // 2) % 2, col % 2
    parity = row % 2
    group = along * 2 + core
    partner = layer * SIDES + (side + 1 - 2 * parity)
    beside = layer * SIDES + (SIDES - 1 - side)
    has_down, has_up = layer > 0, layer < LAYERS - 1
    down, up = row - SIDES, row + SIDES

    place = moved_to(row)
    sends_flipped = crosses(place)
    main = jnp.where(col == 0, 1, core)
    edge_col = (col == 0) | (col == 15)
    mate_col = col + 1 - 2 * core
    mate_place = place + 1 - 2 * (place % 2)

    def left_target(half, reach):
        return (2 * col + half, 4 * (layer // 2) + 2 * reach + layer % 2)

    def left_source(index):
        return (SIDES * group + index, row // 2)

    def peer(step):
        number = (group + step) % 8
        return (row, 4 * (number // 2) + 2 * far + number % 2)

    def same(device):
        return (device[0] == row) & (device[1] == col)

    barrier = pltpu.get_barrier_semaphore()

    def greet(device):
        pl.semaphore_signal(barrier, inc=1, device_id=device, device_id_type=MESH)

    expected = 2 + 7
    greet((partner, col))
    greet((beside, col))
    for step in range(1, 8):
        greet(peer(step))
    pl.when(has_down)(lambda: greet((down, col)))
    pl.when(has_up)(lambda: greet((up, col)))
    expected += has_down.astype(jnp.int32) + has_up.astype(jnp.int32)
    for index in range(SIDES):
        device = left_source(index)
        pl.when(jnp.logical_not(same(device)))(functools.partial(greet, device))
    for half in range(2):
        for reach in range(2):
            expected += 1 - same(left_target(half, reach)).astype(jnp.int32)
    row_source = came_from(row)
    partner_source = came_from(partner)
    greet((row_source, mate_col))
    greet((partner_source, mate_col))
    expected += 2
    for origin in (row_source, partner_source):
        pl.when(edge_col & (origin != row))(functools.partial(greet, (origin, col)))
    for target in (place, mate_place):
        expected += (edge_col & (target != row)).astype(jnp.int32)
    far_place = 2 * col + core
    pl.when(jnp.logical_not(edge_col))(lambda: greet((came_from(far_place), row_source // 2)))
    expected += 2 * sends_flipped.astype(jnp.int32)
    pl.semaphore_wait(barrier, expected)

    def remote(source, target, send_sem, recv_sem, device):
        return pltpu.make_async_remote_copy(
            src_ref=source, dst_ref=target, send_sem=send_sem, recv_sem=recv_sem,
            device_id=device, device_id_type=MESH,
        )

    def arrived(ref, sem):
        remote(ref, ref, sem, sem, (partner, col)).wait_recv()

    def left_copy(half, reach):
        return remote(
            turn.at[:, :, pl.ds(half * ORDER, ORDER)], left.at[:, layer, side],
            left_out.at[half, reach], left_sem.at[side], left_target(half, reach),
        )

    for half in range(2):
        for reach in range(2):
            is_self = same(left_target(half, reach))

            @pl.when(is_self)
            def _():
                pltpu.make_async_copy(
                    turn.at[:, :, pl.ds(half * ORDER, ORDER)], left.at[:, layer, side],
                    left_sem.at[side],
                ).start()

            pl.when(jnp.logical_not(is_self))(left_copy(half, reach).start)

    def side_copy(source, number, which):
        return remote(
            source, right.at[:, number, side], side_out.at[number, which],
            right_sem.at[number, side], (beside if which else partner, col),
        )

    partner_side = side + 1 - 2 * parity

    def relay_copy(number):
        slot = right.at[:, number, partner_side]
        return remote(
            slot, slot, relay_out.at[number], right_sem.at[number, partner_side], (beside, col)
        )

    def up_copy(source, number):
        return remote(
            source, right.at[:, number, side], chain_out.at[number, 0],
            right_sem.at[number, side], (up, col),
        )

    def down_copy(source, number):
        return remote(
            source, right.at[:, number, side], chain_out.at[number, 1],
            right_sem.at[number, side], (down, col),
        )

    pl.when(has_up)(lambda: up_copy(turn, layer).start())
    pl.when(has_down)(lambda: down_copy(turn, layer).start())
    for which in range(2):
        side_copy(turn, layer, which).start()
    other_copy = remote(tile, other, other_out, other_sem, (partner, col))
    other_copy.start()
    own_copy = pltpu.make_async_copy(turn, right.at[:, layer, side], own_sem)
    own_copy.start()

    def spread_copy(step):
        return remote(
            left.at[:, group], left.at[:, group], spread_out.at[step], spread_sem.at[group],
            peer(step),
        )

    for index in range(SIDES):
        arrived(left.at[:, group, index], left_sem.at[index])
    for step in range(1, 8):
        spread_copy(step).start()

    def relay(number):
        arrived(right.at[:, number, partner_side], right_sem.at[number, partner_side])
        relay_copy(number).start()

    relay(layer)

    @pl.loop(0, LAYERS - 1)
    def _(step):
        lower, upper = layer - 1 - step, layer + 1 + step

        @pl.when(lower >= 0)
        def _():
            slot = right.at[:, lower, side]
            arrived(slot, right_sem.at[lower, side])
            pl.when(has_up)(lambda: up_copy(slot, lower).start())
            side_copy(slot, lower, 1).start()
            side_copy(slot, lower, 0).start()

        @pl.when(upper < LAYERS)
        def _():
            slot = right.at[:, upper, side]
            arrived(slot, right_sem.at[upper, side])
            pl.when(has_down)(lambda: down_copy(slot, upper).start())
            side_copy(slot, upper, 1).start()
            side_copy(slot, upper, 0).start()

        pl.when(lower >= 0)(lambda: relay(lower))
        pl.when(upper < LAYERS)(lambda: relay(upper))

    for step in range(1, 8):
        number = (group + step) % 8
        arrived(left.at[:, number], spread_sem.at[number])
    for turn_index in range(ROUNDS):
        for half in range(2):
            part = left[turn_index, 4 * half:4 * half + 4].reshape(ORDER, ORDER)
            high, low = split(part.T)
            left_high[turn_index, half] = high
            left_low[turn_index, half] = low

    def left_of(turn_index, half):
        return left_high[turn_index, half], left_low[turn_index, half]

    arrived(other, other_sem)

    @pl.loop(0, 3)
    def _(step):
        columns = pl.ds(pl.multiple_of(step * 256, 256), 256)
        total = product(left_of(0, parity), split(tile[:, columns]))
        total += product(left_of(0, 1 - parity), split(other[:, columns]))
        mid_high[:, columns], mid_low[:, columns] = split(total)

    own_copy.wait()

    @pl.loop(0, LAYERS)
    def _(number):
        arrived(right.at[:, number, beside % SIDES], right_sem.at[number, beside % SIDES])
        opposite = (side + 2) % SIDES
        arrived(right.at[:, number, opposite], right_sem.at[number, opposite])

    def block_copy(half, which):
        target = mate_place if which else place
        slot = jnp.where(col == 0, 0, core)
        index = place % 2
        return remote(
            block.at[half], fresh.at[index, slot], block_out.at[0, which],
            fresh_sem.at[index, slot], (target, mate_col),
        )

    def edge_copy(half, which):
        target = mate_place if which else place
        slot = jnp.where(col == 0, 0, 1)
        index = place % 2
        return remote(
            block.at[half], fresh.at[index, slot], block_out.at[1, which],
            fresh_sem.at[index, slot], (target, col),
        )

    def flipped_copy(half):
        target = moved_to(2 * col + half)
        return remote(
            flipped.at[half], fresh.at[target % 2, place % 2], flipped_out.at[half],
            fresh_sem.at[target % 2, place % 2], (target, place // 2),
        )

    def is_self(which):
        return (mate_place if which else place) == row

    for half in range(2):
        on_edge = edge_col & (main != half)

        @pl.when((main == half) | edge_col | sends_flipped)
        def _():
            columns = pl.ds(half * ORDER, ORDER)
            turned = right[0, :, :, :, columns].reshape(PAIR, ORDER)
            value = product((mid_high[...], mid_low[...]), split(turned))
            block[half] = value

            @pl.when(sends_flipped)
            def _():
                flipped[half] = value.T
                flipped_copy(half).start()

            @pl.when(main == half)
            def _():
                block_copy(half, 0).start()
                block_copy(half, 1).start()

            for which in range(2):
                pl.when(on_edge & jnp.logical_not(is_self(which)))(edge_copy(half, which).start)

                @pl.when(on_edge & is_self(which))
                def _():
                    slot = jnp.where(col == 0, 0, 1)
                    pltpu.make_async_copy(
                        block.at[half], fresh.at[place % 2, slot],
                        fresh_sem.at[place % 2, slot],
                    ).start()

    far_slot = jnp.where(col == 0, 1, jnp.where(col == 15, 0, core))
    near_slot = 1 - far_slot
    inner = jnp.logical_not(edge_col)

    def arrive_fresh(index, slot):
        arrived(fresh.at[index, slot], fresh_sem.at[index, slot])

    def second_left(slot):
        total = product(left_of(1, 0), split(fresh[0, slot]))
        total += product(left_of(1, 1), split(fresh[1, slot]))
        columns = pl.ds(pl.multiple_of(slot * ORDER, 128), ORDER)
        mid_high[:, columns], mid_low[:, columns] = split(total)

    arrive_fresh(parity, near_slot)
    arrive_fresh(1 - parity, near_slot)
    second_left(near_slot)
    arrive_fresh(parity, far_slot)
    pass_copy = remote(
        fresh.at[parity, far_slot], fresh.at[parity, far_slot], pass_out,
        fresh_sem.at[parity, far_slot], (partner, col),
    )
    pl.when(inner)(pass_copy.start)
    arrive_fresh(1 - parity, far_slot)
    second_left(far_slot)

    @pl.loop(0, 3)
    def _(step):
        columns = pl.ds(pl.multiple_of(step * 256, 256), 256)
        turned = right[1, :, :, :, columns].reshape(PAIR, 256)
        out[:, columns] = product((mid_high[...], mid_low[...]), split(turned))

    for half in range(2):
        for reach in range(2):
            device = left_target(half, reach)
            pl.when(jnp.logical_not(same(device)))(left_copy(half, reach).wait_send)
    for step in range(1, 8):
        spread_copy(step).wait_send()

    @pl.loop(0, LAYERS)
    def _(number):
        slot = right.at[:, number, side]
        pl.when(has_up & (number <= layer))(lambda: up_copy(slot, number).wait_send())
        pl.when(has_down & (number >= layer))(lambda: down_copy(slot, number).wait_send())
        side_copy(slot, number, 0).wait_send()
        side_copy(slot, number, 1).wait_send()
        relay_copy(number).wait_send()

    other_copy.wait_send()
    for half in range(2):
        pl.when(sends_flipped)(flipped_copy(half).wait_send)
    for which in range(2):
        block_copy(0, which).wait_send()
        pl.when(edge_col & jnp.logical_not(is_self(which)))(edge_copy(0, which).wait_send)
    pl.when(inner)(pass_copy.wait_send)


def per_device(covariance, rotations, flips):
    shard = rotations[:, 0]
    own_flip = flips[:, lax.axis_index("col")]
    traded = jnp.concatenate([shard[:, :, ORDER:], shard[:, :, :ORDER]], 2)
    turn = jnp.where((own_flip == 1)[:, None, None], traded, shard)
    dma = pltpu.SemaphoreType.DMA
    return pl.pallas_call(
        kernel,
        out_shape=jax.ShapeDtypeStruct((ORDER, PAIR), jnp.float32),
        in_specs=[pl.BlockSpec(memory_space=pltpu.VMEM)] * 2,
        out_specs=pl.BlockSpec(memory_space=pltpu.VMEM),
        scratch_shapes=[
            pltpu.VMEM((ROUNDS, LAYERS, SIDES, PIECE, PAIR), jnp.float32),
            pltpu.VMEM((ROUNDS, LAYERS, SIDES, PIECE, ORDER), jnp.float32),
            pltpu.VMEM((ORDER, PAIR), jnp.float32),
            pltpu.VMEM((2, 2, ORDER, ORDER), jnp.float32),
            pltpu.VMEM((2, ORDER, ORDER), jnp.float32),
            pltpu.VMEM((2, ORDER, ORDER), jnp.float32),
            pltpu.VMEM((ROUNDS, 2, ORDER, ORDER), jnp.bfloat16),
            pltpu.VMEM((ROUNDS, 2, ORDER, ORDER), jnp.bfloat16),
            pltpu.VMEM((ORDER, PAIR), jnp.bfloat16),
            pltpu.VMEM((ORDER, PAIR), jnp.bfloat16),
            dma,
            dma,
            dma((LAYERS, SIDES)),
            dma((SIDES,)),
            dma((LAYERS,)),
            dma((2, 2)),
            dma((LAYERS, 2)),
            dma((LAYERS, 2)),
            dma((LAYERS,)),
            dma((2, 2)),
            dma((8,)),
            dma,
            dma((2, 2)),
            dma((2,)),
            dma,
        ],
        compiler_params=pltpu.CompilerParams(
            collective_id=0, has_side_effects=True, vmem_limit_bytes=48 * 2**20
        ),
        cost_estimate=pl.CostEstimate(
            flops=12 * ORDER * PAIR * PAIR, bytes_accessed=3 * 2**20, transcendentals=0
        ),
    )(covariance, turn)


def solution(mesh):
    placed = (P("row", "col"), P(None, "col", "row", None), P())
    return jax.shard_map(
        per_device, mesh=mesh, in_specs=placed, out_specs=P("row", "col"), check_vma=False
    )
```

```python
import functools

import jax
import jax.numpy as jnp
from jax import lax
from jax.experimental import pallas as pl
from jax.experimental.pallas import tpu as pltpu
from jax.sharding import PartitionSpec as P

ROUNDS = 2
ORDER = 384
PAIR = 768
LAYERS = 8
SIDES = 4
PIECE = 24
CHUNKS = 4
CHUNK = 96
MESH = pl.DeviceIdType.MESH


def split(value):
    high = value.astype(jnp.bfloat16)
    return high, (value - high.astype(jnp.float32)).astype(jnp.bfloat16)


def product(first, second):
    one = functools.partial(jnp.dot, preferred_element_type=jnp.float32)
    return one(first[0], second[0]) + (one(first[0], second[1]) + one(first[1], second[0]))


def moved_to(place):
    even = jnp.where(place == 0, 0, jnp.where(place == 30, 31, place + 2))
    return jnp.where(place % 2 == 0, even, jnp.where(place == 1, 2, place - 2))


def came_from(place):
    even = jnp.where(place == 0, 0, jnp.where(place == 2, 1, place - 2))
    return jnp.where(place % 2 == 0, even, jnp.where(place == 31, 30, place + 2))


def kernel(
    tile, turn, out, right, left, both, fresh, block, stage, left_high, left_low, mid_high,
    mid_low, passing, tile_sem, own_sem, pair_sem, right_sem, left_sem, mirror_sem, spread_sem, both_sem,
    fresh_sem, passing_sem,
    out_sem, left_out, mirror_out, spread_out, pair_out, both_out, chain_out, across_out,
    mate_out, mate_both_out, block_out, mate_fresh_out, final_out, passing_out,
):
    row, col = lax.axis_index("row"), lax.axis_index("col")
    layer, side = row // SIDES, row % SIDES
    along, far, core = col // 4, (col // 2) % 2, col % 2
    parity, half_side = row % 2, side // 2
    pair, target_pair = row // 2, 2 * (col // 2) + parity
    is_main = core == parity
    is_helper = core != parity
    mate_col = col + 1 - 2 * core
    partner_row = row + 1 - 2 * parity
    across_row = layer * SIDES + (side + 2) % SIDES
    has_down, has_up = layer > 0, layer < LAYERS - 1
    down, up = row - SIDES, row + SIDES
    mate, partner, across = (row, mate_col), (partner_row, col), (across_row, col)
    diagonal = (partner_row, mate_col)

    def same(device):
        return (device[0] == row) & (device[1] == col)

    def left_target(half, reach):
        return (2 * col + layer % 2, 4 * (layer // 2) + 2 * reach + half)

    def left_source(index):
        return (SIDES * (2 * along + parity) + index, pair)

    def peer(step):
        return (row, (col + 4 * step) % 16)

    far_half = jnp.where(target_pair % 2 == 0, 1, 0)
    far_slot = 1 - far_half

    def inside(pair_col):
        return (pair_col != 0) & (pair_col != 15)

    def target_of(old_row, old_col):
        new_row, new_col = moved_to(old_row), moved_to(old_col)
        pair_col = new_col // 2
        return (2 * (new_row // 2) + pair_col % 2, 2 * (pair_col // 2) + new_row % 2)

    def relayed(old_row, pair_col, is_far):
        return is_far & inside(pair_col) & (old_row % 2 == (old_row // 2) % 2)

    def turned_layer(number, half_z):
        wraps = (number < 0) | (number >= LAYERS)
        return (number + LAYERS) % LAYERS, jnp.where(wraps, 1 - half_z, half_z)

    def relay_of(old_row, pair_col):
        odd = (old_row // 2) % 2
        number, half_z = turned_layer(old_row // 4 + 2 * odd - 1, (pair_col // 2) % 2)
        return (
            number * SIDES + 2 * odd + pair_col % 2,
            4 * (pair_col // 4) + 2 * half_z + 1 - pair_col % 2,
        )

    def block_target(half):
        old_row = 2 * pair + core
        end = target_of(old_row, 2 * target_pair + half)
        through = relayed(old_row, target_pair, half == far_half)
        stop = relay_of(old_row, target_pair)
        return tuple(jnp.where(through, one, other) for one, other in zip(stop, end))

    def block_source(slot):
        old_row, old_col = came_from(2 * pair + core), came_from(2 * target_pair + slot)
        pair_col = old_col // 2
        start = (2 * (old_row // 2) + pair_col % 2, 2 * (pair_col // 2) + old_row % 2)
        far = jnp.where(pair_col % 2 == 0, 1, 0)
        through = relayed(old_row, pair_col, old_col % 2 == far)
        stop = relay_of(old_row, pair_col)
        return tuple(jnp.where(through, one, other) for one, other in zip(stop, start))

    relay_layer, relay_far = turned_layer(layer + 1 - 2 * half_side, far)
    relay_pair, relay_col = 2 * relay_layer + half_side, 4 * along + 2 * relay_far + parity
    relays = is_helper & inside(relay_col)
    relay_source = (relay_layer * SIDES + side, 4 * along + 2 * relay_far + half_side)
    own_row = 2 * pair + core
    uses_relay = relayed(own_row, target_pair, jnp.bool_(True))
    relay_old = (2 * relay_pair + half_side, 2 * relay_col + far_half)
    relay_target = target_of(*relay_old)

    barrier = pltpu.get_barrier_semaphore()

    def greet(device, when=None):
        def signal():
            pl.semaphore_signal(barrier, inc=1, device_id=device, device_id_type=MESH)

        if when is None:
            signal()
        else:
            pl.when(when)(signal)

    def count(flag):
        return flag.astype(jnp.int32)

    expected = 6
    for device in (mate, partner, across, peer(1), peer(2), peer(3)):
        greet(device)
    for device, when in (
        (diagonal, is_helper), ((up, col), has_up), ((down, col), has_down)
    ):
        greet(device, when)
        expected += count(when)
    for index in range(SIDES):
        device = left_source(index)
        greet(device, jnp.logical_not(same(device)))
    for half in range(2):
        for reach in range(2):
            expected += 1 - count(same(left_target(half, reach)))
    for slot in range(2):
        device = block_source(slot)
        greet(device, jnp.logical_not(same(device)))
        expected += 1 - count(same(block_target(slot)))
    greet(relay_source, relays)
    expected += count(relays)
    pl.semaphore_wait(barrier, expected)

    def remote(source, target, send_sem, recv_sem, device):
        return pltpu.make_async_remote_copy(
            src_ref=source, dst_ref=target, send_sem=send_sem, recv_sem=recv_sem,
            device_id=device, device_id_type=MESH,
        )

    def arrived(ref, sem):
        remote(ref, ref, sem, sem, partner).wait_recv()

    def left_piece(index, half):
        return turn.at[index, half]

    def left_copy(index, half, reach):
        return remote(
            left_piece(index, half), left.at[index, layer, side], left_out.at[index, half, reach],
            left_sem.at[index, side], left_target(half, reach),
        )

    def left_start(index):
        for half in range(2):
            for reach in range(2):
                here = same(left_target(half, reach))
                pl.when(here)(
                    pltpu.make_async_copy(
                        left_piece(index, half), left.at[index, layer, side],
                        left_sem.at[index, side],
                    ).start
                )
                pl.when(jnp.logical_not(here))(left_copy(index, half, reach).start)

    group = 2 * along + parity

    def mirror_copy(index):
        slot = left.at[index, group]
        return remote(slot, slot, mirror_out.at[index], mirror_sem.at[index], partner)

    def spread_copy(index, which, step):
        number = 2 * along + (parity if which == 0 else 1 - parity)
        slot = left.at[index, number]
        return remote(
            slot, slot, spread_out.at[index, which, step], spread_sem.at[index, number], peer(step)
        )

    def left_mirror(index):
        for number in range(SIDES):
            arrived(left.at[index, group, number], left_sem.at[index, number])
        mirror_copy(index).start()
        for step in range(1, 4):
            spread_copy(index, 0, step).start()

    def left_spread(index):
        arrived(left.at[index, 2 * along + 1 - parity], mirror_sem.at[index])
        for step in range(1, 4):
            spread_copy(index, 1, step).start()

    def left_finish(index):
        for step in range(1, 4):
            for which in range(2):
                number = 2 * ((along + step) % 4) + which
                arrived(left.at[index, number], spread_sem.at[index, number])
        for half in range(2):
            part = left[index, 4 * half:4 * half + 4].reshape(ORDER, ORDER)
            left_high[index, half], left_low[index, half] = split(part.T)

    def slot_of(index, half, number, which):
        return right.at[1, :, number, which] if index else right.at[0, half, number, which]

    def piece_slot(index, half, which):
        rows = pl.ds(pl.multiple_of(PIECE * which, 8), PIECE)
        if index:
            return right.at[1, :, layer, half_side, rows]
        return right.at[0, half, layer, half_side, rows]

    def chunk(ref, index, number):
        return ref.at[index, pl.ds(number * CHUNK, CHUNK)]

    def pair_copy(half):
        return remote(
            turn.at[0, half], piece_slot(0, half, parity), pair_out.at[half], pair_sem.at[half],
            partner,
        )

    def later_copy(device, number):
        return remote(
            turn.at[1], piece_slot(1, 0, parity), pair_out.at[2], pair_sem.at[2 + number], device
        )

    to_mate, to_diagonal = later_copy(mate, 0), later_copy(diagonal, 1)

    def own_piece(half):
        return pltpu.make_async_copy(
            turn.at[0, half], piece_slot(0, half, parity), own_sem.at[half]
        )

    own_tile = pltpu.make_async_copy(tile, both.at[parity], tile_sem)
    mate_tile = remote(tile, both.at[parity], mate_both_out.at[CHUNKS], both_sem.at[CHUNKS], mate)

    def both_copy(number):
        return remote(
            tile.at[pl.ds(number * CHUNK, CHUNK)], chunk(both, parity, number),
            both_out.at[number], both_sem.at[number], partner,
        )

    def mate_both(number):
        slot = chunk(both, 1 - parity, number)
        return remote(slot, slot, mate_both_out.at[number], both_sem.at[number], mate)

    def toward(index, half, number, which, sem, device):
        slot = slot_of(index, half, number, which)
        return remote(slot, slot, sem, right_sem.at[index, half, number, which], device)

    def up_copy(index, half, number):
        return toward(
            index, half, number, half_side, chain_out.at[index, half, number, 0], (up, col)
        )

    def down_copy(index, half, number):
        return toward(
            index, half, number, half_side, chain_out.at[index, half, number, 1], (down, col)
        )

    def across_copy(index, half, number):
        return toward(index, half, number, half_side, across_out.at[index, half, number], across)

    def mate_copy(index, half, number, which):
        return toward(index, half, number, which, mate_out.at[index, half, number, which], mate)

    def wait_right(index, half, number, which):
        arrived(slot_of(index, half, number, which), right_sem.at[index, half, number, which])

    halves = (far_half, 1 - far_half)

    def chain_send(index, half):
        pl.when(has_up)(lambda: up_copy(index, half, layer).start())
        pl.when(has_down)(lambda: down_copy(index, half, layer).start())
        across_copy(index, half, layer).start()
        mate_copy(index, half, layer, half_side).start()

    def chain_step(index, half, step):
        lower, upper = layer - 1 - step, layer + 1 + step

        @pl.when(lower >= 0)
        def _():
            wait_right(index, half, lower, half_side)
            pl.when(has_up)(lambda: up_copy(index, half, lower).start())
            across_copy(index, half, lower).start()
            mate_copy(index, half, lower, half_side).start()

        @pl.when(upper < LAYERS)
        def _():
            wait_right(index, half, upper, half_side)
            pl.when(has_down)(lambda: down_copy(index, half, upper).start())
            across_copy(index, half, upper).start()
            mate_copy(index, half, upper, half_side).start()

    def chain_finish(index, half):
        leads, follows = (is_helper, is_main) if index else (is_main, is_helper)

        @pl.when(leads)
        def _():
            @pl.loop(0, LAYERS)
            def _(number):
                wait_right(index, half, number, 1 - half_side)
                mate_copy(index, half, number, 1 - half_side).start()

        @pl.when(follows)
        def _():
            @pl.loop(0, LAYERS)
            def _(number):
                wait_right(index, half, number, 0)
                wait_right(index, half, number, 1)

    @pl.when(is_helper)
    def _():
        for half in halves:
            pair_copy(half).start()

    left_start(0)

    @pl.when(is_helper)
    def _():
        for number in range(CHUNKS):
            both_copy(number).start()
        to_diagonal.start()
        arrived(piece_slot(1, 0, parity), pair_sem.at[2])
        arrived(piece_slot(1, 0, 1 - parity), pair_sem.at[3])
        chain_send(1, 0)

    @pl.when(is_main)
    def _():
        to_mate.start()
        for half in halves:
            own_piece(half).start()
        for half in halves:
            own_piece(half).wait()
            arrived(piece_slot(0, half, 1 - parity), pair_sem.at[half])
            chain_send(0, half)
        own_tile.start()
        mate_tile.start()

    @pl.loop(0, LAYERS - 1)
    def _(step):
        @pl.when(is_main)
        def _():
            @pl.loop(0, 2)
            def _(turn_half):
                half = jnp.where(turn_half == 0, far_half, 1 - far_half)
                chain_step(0, half, step)

        pl.when(is_helper)(lambda: chain_step(1, 0, step))
        pl.when(step == 2)(lambda: left_mirror(0))
        pl.when(step == 4)(lambda: left_spread(0))

        @pl.when(is_main & (step >= 3))
        def _():
            number = step - 3
            arrived(chunk(both, 1 - parity, number), both_sem.at[number])
            mate_both(number).start()

    left_start(1)

    left_finish(0)

    def left_of(index, half):
        return left_high[index, half], left_low[index, half]

    pl.when(is_main)(own_tile.wait)

    @pl.when(is_helper)
    def _():
        arrived(both.at[parity], both_sem.at[CHUNKS])
        for number in range(CHUNKS):
            arrived(chunk(both, 1 - parity, number), both_sem.at[number])

    @pl.loop(0, 3)
    def _(step):
        columns = pl.ds(pl.multiple_of(step * 256, 256), 256)
        total = product(left_of(0, 0), split(both[0, :, columns]))
        total += product(left_of(0, 1), split(both[1, :, columns]))
        mid_high[:, columns], mid_low[:, columns] = split(total)

    def block_ends(half):
        new_row, new_col = moved_to(2 * pair + core), moved_to(2 * target_pair + half)
        index, slot = new_row % 2, new_col % 2
        return block.at[half], fresh.at[index, slot], fresh_sem.at[index, slot]

    def block_copy(half):
        source, target, sem = block_ends(half)
        return remote(source, target, block_out.at[half, 0], sem, block_target(half))

    def relayed_copy(number):
        rows = pl.ds(number * CHUNK, CHUNK)
        return remote(
            block.at[far_half, rows], passing.at[rows], block_out.at[far_half, number],
            passing_sem.at[number], block_target(far_half),
        )

    def passing_copy(number):
        rows = pl.ds(number * CHUNK, CHUNK)
        index, slot = moved_to(relay_old[0]) % 2, moved_to(relay_old[1]) % 2
        return remote(
            passing.at[rows], fresh.at[index, slot, rows], passing_out.at[number],
            fresh_sem.at[index, slot], relay_target,
        )

    @pl.loop(0, 2)
    def _(step):
        half = jnp.where(step == 0, far_half, 1 - far_half)
        chain_finish(0, half)
        turned = right[0, half].reshape(PAIR, ORDER)
        block[half] = product((mid_high[...], mid_low[...]), split(turned))
        here = same(block_target(half))
        through = uses_relay & (half == far_half)

        @pl.when(through)
        def _():
            for number in range(CHUNKS):
                relayed_copy(number).start()

        plain = jnp.logical_not(here) & jnp.logical_not(through)
        pl.when(plain)(lambda: block_copy(half).start())
        pl.when(here)(lambda: pltpu.make_async_copy(*block_ends(half)).start())

    @pl.when(relays)
    def _():
        for number in range(CHUNKS):
            arrived(passing.at[pl.ds(number * CHUNK, CHUNK)], passing_sem.at[number])
            passing_copy(number).start()

    left_mirror(1)
    left_spread(1)
    chain_finish(1, 0)
    left_finish(1)

    def arrive_fresh(index, slot):
        arrived(fresh.at[index, slot], fresh_sem.at[index, slot])

    def mate_fresh(slot):
        ref = fresh.at[core, slot]
        return remote(ref, ref, mate_fresh_out.at[slot], fresh_sem.at[core, slot], mate)

    @pl.loop(0, 2)
    def _(step):
        slot = jnp.where(step == 0, 1 - far_slot, far_slot)
        arrive_fresh(core, slot)
        mate_fresh(slot).start()
        arrive_fresh(1 - core, slot)
        total = product(left_of(1, 0), split(fresh[0, slot]))
        total += product(left_of(1, 1), split(fresh[1, slot]))
        columns = pl.ds(pl.multiple_of(slot * ORDER, 128), ORDER)
        mid_high[:, columns], mid_low[:, columns] = split(total)

    def final_copy(number):
        columns = pl.ds(number * ORDER, ORDER)
        return remote(
            stage.at[:, columns], out.at[:, columns], final_out.at[number], out_sem.at[number],
            diagonal,
        )

    for number in range(2):
        columns = pl.ds(number * ORDER, ORDER)
        turned = right[1, number].reshape(PAIR, ORDER)
        value = product((mid_high[...], mid_low[...]), split(turned))

        @pl.when(is_main)
        def _():
            out[:, columns] = value

        @pl.when(is_helper)
        def _():
            stage[:, columns] = value
            final_copy(number).start()

    for index in range(ROUNDS):
        for half in range(2):
            for reach in range(2):
                device = left_target(half, reach)
                pl.when(jnp.logical_not(same(device)))(left_copy(index, half, reach).wait_send)
        mirror_copy(index).wait_send()
        for step in range(1, 4):
            spread_copy(index, 0, step).wait_send()
            spread_copy(index, 1, step).wait_send()
    for half in range(2):
        through = uses_relay & (half == far_half)
        plain = jnp.logical_not(same(block_target(half))) & jnp.logical_not(through)
        pl.when(plain)(block_copy(half).wait_send)
        mate_fresh(half).wait_send()

    @pl.when(is_helper)
    def _():
        for half in range(2):
            pair_copy(half).wait_send()
        to_diagonal.wait_send()
        for number in range(CHUNKS):
            both_copy(number).wait_send()

    @pl.when(is_main)
    def _():
        mate_tile.wait_send()
        for number in range(CHUNKS):
            mate_both(number).wait_send()

        to_mate.wait_send()

    def chain_left(index, half):
        @pl.loop(0, LAYERS)
        def _(number):
            rises, falls = has_up & (number <= layer), has_down & (number >= layer)
            pl.when(rises)(lambda: up_copy(index, half, number).wait_send())
            pl.when(falls)(lambda: down_copy(index, half, number).wait_send())
            across_copy(index, half, number).wait_send()
            mate_copy(index, half, number, 0).wait_send()
            mate_copy(index, half, number, 1).wait_send()

    pl.when(is_main)(lambda: chain_left(0, 0))
    pl.when(is_main)(lambda: chain_left(0, 1))
    pl.when(is_helper)(lambda: chain_left(1, 0))

    for number in range(CHUNKS):
        pl.when(uses_relay)(relayed_copy(number).wait_send)
        pl.when(relays)(passing_copy(number).wait_send)

    @pl.when(is_helper)
    def _():
        for number in range(2):
            arrived(out.at[:, pl.ds(number * ORDER, ORDER)], out_sem.at[number])
            final_copy(number).wait_send()


def per_device(covariance, rotations, flips):
    shard = rotations[:, 0]
    own_flip = flips[:, lax.axis_index("col")]
    halves = jnp.stack([shard[:, :, :ORDER], shard[:, :, ORDER:]], 1)
    turn = jnp.where((own_flip == 1)[:, None, None, None], halves[:, ::-1], halves)
    dma = pltpu.SemaphoreType.DMA
    return pl.pallas_call(
        kernel,
        out_shape=jax.ShapeDtypeStruct((ORDER, PAIR), jnp.float32),
        in_specs=[pl.BlockSpec(memory_space=pltpu.VMEM)] * 2,
        out_specs=pl.BlockSpec(memory_space=pltpu.VMEM),
        scratch_shapes=[
            pltpu.VMEM((ROUNDS, 2, LAYERS, 2, 2 * PIECE, ORDER), jnp.float32),
            pltpu.VMEM((ROUNDS, LAYERS, SIDES, PIECE, ORDER), jnp.float32),
            pltpu.VMEM((2, ORDER, PAIR), jnp.float32),
            pltpu.VMEM((2, 2, ORDER, ORDER), jnp.float32),
            pltpu.VMEM((2, ORDER, ORDER), jnp.float32),
            pltpu.VMEM((ORDER, PAIR), jnp.float32),
            pltpu.VMEM((ROUNDS, 2, ORDER, ORDER), jnp.bfloat16),
            pltpu.VMEM((ROUNDS, 2, ORDER, ORDER), jnp.bfloat16),
            pltpu.VMEM((ORDER, PAIR), jnp.bfloat16),
            pltpu.VMEM((ORDER, PAIR), jnp.bfloat16),
            pltpu.VMEM((ORDER, ORDER), jnp.float32),
            dma,
            dma((2,)),
            dma((4,)),
            dma((ROUNDS, 2, LAYERS, 2)),
            dma((ROUNDS, SIDES)),
            dma((ROUNDS,)),
            dma((ROUNDS, 8)),
            dma((CHUNKS + 1,)),
            dma((2, 2)),
            dma((CHUNKS,)),
            dma((2,)),
            dma((ROUNDS, 2, 2)),
            dma((ROUNDS,)),
            dma((ROUNDS, 2, 4)),
            dma((3,)),
            dma((CHUNKS,)),
            dma((ROUNDS, 2, LAYERS, 2)),
            dma((ROUNDS, 2, LAYERS)),
            dma((ROUNDS, 2, LAYERS, 2)),
            dma((CHUNKS + 1,)),
            dma((2, CHUNKS)),
            dma((2,)),
            dma((2,)),
            dma((CHUNKS,)),
        ],
        compiler_params=pltpu.CompilerParams(
            collective_id=0, has_side_effects=True, vmem_limit_bytes=48 * 2**20
        ),
        cost_estimate=pl.CostEstimate(
            flops=12 * ORDER * PAIR * PAIR, bytes_accessed=3 * 2**20, transcendentals=0
        ),
    )(covariance, turn)


def solution(mesh):
    placed = (P("row", "col"), P(None, "col", "row", None), P())
    return jax.shard_map(
        per_device, mesh=mesh, in_specs=placed, out_specs=P("row", "col"), check_vma=False
    )
```

```python
import functools

import jax
import jax.numpy as jnp
from jax import lax
from jax.experimental import pallas as pl
from jax.experimental.pallas import tpu as pltpu
from jax.sharding import PartitionSpec as P

ROUNDS = 2
ORDER = 384
PAIR = 768
LAYERS = 8
SIDES = 4
PIECE = 24
CHUNKS = 4
CHUNK = 96
MESH = pl.DeviceIdType.MESH


def split(value):
    high = value.astype(jnp.bfloat16)
    return high, (value - high.astype(jnp.float32)).astype(jnp.bfloat16)


def product(first, second):
    one = functools.partial(jnp.dot, preferred_element_type=jnp.float32)
    return one(first[0], second[0]) + (one(first[0], second[1]) + one(first[1], second[0]))


def moved_to(place):
    even = jnp.where(place == 0, 0, jnp.where(place == 30, 31, place + 2))
    return jnp.where(place % 2 == 0, even, jnp.where(place == 1, 2, place - 2))


def came_from(place):
    even = jnp.where(place == 0, 0, jnp.where(place == 2, 1, place - 2))
    return jnp.where(place % 2 == 0, even, jnp.where(place == 31, 30, place + 2))


def kernel(
    tile, turn, out, right, left, both, fresh, block, stage, left_high, left_low, mid_high,
    mid_low, passing, tile_sem, own_sem, pair_sem, right_sem, left_sem, mirror_sem, spread_sem, both_sem,
    fresh_sem, passing_sem,
    out_sem, left_out, mirror_out, spread_out, pair_out, both_out, chain_out, across_out,
    mate_out, mate_both_out, block_out, mate_fresh_out, final_out, passing_out,
):
    row, col = lax.axis_index("row"), lax.axis_index("col")
    layer, side = row // SIDES, row % SIDES
    along, far, core = col // 4, (col // 2) % 2, col % 2
    parity, half_side = row % 2, side // 2
    pair, target_pair = row // 2, 2 * (col // 2) + parity
    is_main = core == parity
    is_helper = core != parity
    mate_col = col + 1 - 2 * core
    partner_row = row + 1 - 2 * parity
    across_row = layer * SIDES + (side + 2) % SIDES
    has_down, has_up = layer > 0, layer < LAYERS - 1
    down, up = row - SIDES, row + SIDES
    mate, partner, across = (row, mate_col), (partner_row, col), (across_row, col)
    diagonal = (partner_row, mate_col)

    def same(device):
        return (device[0] == row) & (device[1] == col)

    def left_target(half, reach):
        return (2 * col + layer % 2, 4 * side + 2 * reach + half)

    def left_source(index):
        return (SIDES * (2 * index + parity) + along, pair)

    def peer(step):
        return (row, (col + 4 * step) % 16)

    far_half = jnp.where(target_pair % 2 == 0, 1, 0)
    far_slot = 1 - far_half

    def inside(pair_col):
        return (pair_col != 0) & (pair_col != 15)

    def target_of(old_row, old_col):
        new_row, new_col = moved_to(old_row), moved_to(old_col)
        pair_col = new_col // 2
        return (2 * (new_row // 2) + pair_col % 2, 2 * (pair_col // 2) + new_row % 2)

    def relayed(old_row, pair_col, is_far):
        return is_far & inside(pair_col) & (old_row % 2 == (old_row // 2) % 2)

    def turned_layer(number, half_z):
        wraps = (number < 0) | (number >= LAYERS)
        return (number + LAYERS) % LAYERS, jnp.where(wraps, 1 - half_z, half_z)

    def relay_of(old_row, pair_col):
        odd = (old_row // 2) % 2
        number, half_z = turned_layer(old_row // 4 + 2 * odd - 1, (pair_col // 2) % 2)
        return (
            number * SIDES + 2 * odd + pair_col % 2,
            4 * (pair_col // 4) + 2 * half_z + 1 - pair_col % 2,
        )

    def block_target(half):
        old_row = 2 * pair + core
        end = target_of(old_row, 2 * target_pair + half)
        through = relayed(old_row, target_pair, half == far_half)
        stop = relay_of(old_row, target_pair)
        return tuple(jnp.where(through, one, other) for one, other in zip(stop, end))

    def block_source(slot):
        old_row, old_col = came_from(2 * pair + core), came_from(2 * target_pair + slot)
        pair_col = old_col // 2
        start = (2 * (old_row // 2) + pair_col % 2, 2 * (pair_col // 2) + old_row % 2)
        far = jnp.where(pair_col % 2 == 0, 1, 0)
        through = relayed(old_row, pair_col, old_col % 2 == far)
        stop = relay_of(old_row, pair_col)
        return tuple(jnp.where(through, one, other) for one, other in zip(stop, start))

    relay_layer, relay_far = turned_layer(layer + 1 - 2 * half_side, far)
    relay_pair, relay_col = 2 * relay_layer + half_side, 4 * along + 2 * relay_far + parity
    relays = is_helper & inside(relay_col)
    relay_source = (relay_layer * SIDES + side, 4 * along + 2 * relay_far + half_side)
    own_row = 2 * pair + core
    uses_relay = relayed(own_row, target_pair, jnp.bool_(True))
    relay_old = (2 * relay_pair + half_side, 2 * relay_col + far_half)
    relay_target = target_of(*relay_old)

    barrier = pltpu.get_barrier_semaphore()

    def greet(device, when=None):
        def signal():
            pl.semaphore_signal(barrier, inc=1, device_id=device, device_id_type=MESH)

        if when is None:
            signal()
        else:
            pl.when(when)(signal)

    def count(flag):
        return flag.astype(jnp.int32)

    expected = 6
    for device in (mate, partner, across, peer(1), peer(2), peer(3)):
        greet(device)
    for device, when in (
        (diagonal, is_helper), ((up, col), has_up), ((down, col), has_down)
    ):
        greet(device, when)
        expected += count(when)
    for index in range(SIDES):
        device = left_source(index)
        greet(device, jnp.logical_not(same(device)))
    for half in range(2):
        for reach in range(2):
            expected += 1 - count(same(left_target(half, reach)))
    for slot in range(2):
        device = block_source(slot)
        greet(device, jnp.logical_not(same(device)))
        expected += 1 - count(same(block_target(slot)))
    greet(relay_source, relays)
    expected += count(relays)
    pl.semaphore_wait(barrier, expected)

    def remote(source, target, send_sem, recv_sem, device):
        return pltpu.make_async_remote_copy(
            src_ref=source, dst_ref=target, send_sem=send_sem, recv_sem=recv_sem,
            device_id=device, device_id_type=MESH,
        )

    def arrived(ref, sem):
        remote(ref, ref, sem, sem, partner).wait_recv()

    def left_piece(index, half):
        return turn.at[index, half]

    def left_piece_slot(index):
        return left.at[index, side, layer % 2, layer // 2]

    def left_copy(index, half, reach):
        return remote(
            left_piece(index, half), left_piece_slot(index), left_out.at[index, half, reach],
            left_sem.at[index, layer // 2], left_target(half, reach),
        )

    def left_start(index):
        for half in range(2):
            for reach in range(2):
                here = same(left_target(half, reach))
                pl.when(here)(
                    pltpu.make_async_copy(
                        left_piece(index, half), left_piece_slot(index),
                        left_sem.at[index, layer // 2],
                    ).start
                )
                pl.when(jnp.logical_not(here))(left_copy(index, half, reach).start)

    def mirror_copy(index, number):
        slot = left.at[index, along, parity, number]
        return remote(
            slot, slot, mirror_out.at[index, number], mirror_sem.at[index, number], partner
        )

    def spread_copy(index, which, number, step):
        half = parity if which == 0 else 1 - parity
        slot, sem = left.at[index, along, half, number], spread_sem.at[index, along, half]
        return remote(slot, slot, spread_out.at[index, which, number, step], sem, peer(step))

    def left_pass(index, number):
        arrived(left.at[index, along, parity, number], left_sem.at[index, number])
        mirror_copy(index, number).start()
        for step in range(1, 4):
            spread_copy(index, 0, number, step).start()

    def left_relay(index, number):
        arrived(left.at[index, along, 1 - parity, number], mirror_sem.at[index, number])
        for step in range(1, 4):
            spread_copy(index, 1, number, step).start()

    def left_hooks(index, step):
        pl.when((step >= 1) & (step < 5))(lambda: left_pass(index, step - 1))
        pl.when(step >= 3)(lambda: left_relay(index, step - 3))

    def left_finish(index):
        for step in range(1, 4):
            for which in range(2):
                number = (along + step) % 4
                arrived(left.at[index, number, which], spread_sem.at[index, number, which])
        for half in range(2):
            pieces = [
                left[index, y, z % 2, z // 2]
                for z in range(4 * half, 4 * half + 4) for y in range(SIDES)
            ]
            part = jnp.concatenate(pieces, 0)
            left_high[index, half], left_low[index, half] = split(part.T)

    def slot_of(index, half, number, which):
        return right.at[1, :, number, which] if index else right.at[0, half, number, which]

    def piece_slot(index, half, which):
        rows = pl.ds(pl.multiple_of(PIECE * which, 8), PIECE)
        if index:
            return right.at[1, :, layer, half_side, rows]
        return right.at[0, half, layer, half_side, rows]

    def chunk(ref, index, number):
        return ref.at[index, pl.ds(number * CHUNK, CHUNK)]

    def pair_copy(half):
        return remote(
            turn.at[0, half], piece_slot(0, half, parity), pair_out.at[half], pair_sem.at[half],
            partner,
        )

    def later_copy(device, number):
        return remote(
            turn.at[1], piece_slot(1, 0, parity), pair_out.at[2], pair_sem.at[2 + number], device
        )

    to_mate, to_diagonal = later_copy(mate, 0), later_copy(diagonal, 1)

    def own_piece(half):
        return pltpu.make_async_copy(
            turn.at[0, half], piece_slot(0, half, parity), own_sem.at[half]
        )

    own_tile = pltpu.make_async_copy(tile, both.at[parity], tile_sem)
    mate_tile = remote(tile, both.at[parity], mate_both_out.at[CHUNKS], both_sem.at[CHUNKS], mate)

    def both_copy(number):
        return remote(
            tile.at[pl.ds(number * CHUNK, CHUNK)], chunk(both, parity, number),
            both_out.at[number], both_sem.at[number], partner,
        )

    def mate_both(number):
        slot = chunk(both, 1 - parity, number)
        return remote(slot, slot, mate_both_out.at[number], both_sem.at[number], mate)

    def toward(index, half, number, which, sem, device):
        slot = slot_of(index, half, number, which)
        return remote(slot, slot, sem, right_sem.at[index, half, number, which], device)

    def up_copy(index, half, number):
        return toward(
            index, half, number, half_side, chain_out.at[index, half, number, 0], (up, col)
        )

    def down_copy(index, half, number):
        return toward(
            index, half, number, half_side, chain_out.at[index, half, number, 1], (down, col)
        )

    def across_copy(index, half, number):
        return toward(index, half, number, half_side, across_out.at[index, half, number], across)

    def mate_copy(index, half, number, which):
        return toward(index, half, number, which, mate_out.at[index, half, number, which], mate)

    def wait_right(index, half, number, which):
        arrived(slot_of(index, half, number, which), right_sem.at[index, half, number, which])

    halves = (far_half, 1 - far_half)

    def chain_send(index, half):
        pl.when(has_up)(lambda: up_copy(index, half, layer).start())
        pl.when(has_down)(lambda: down_copy(index, half, layer).start())
        across_copy(index, half, layer).start()
        mate_copy(index, half, layer, half_side).start()

    def chain_step(index, half, step):
        lower, upper = layer - 1 - step, layer + 1 + step

        @pl.when(lower >= 0)
        def _():
            wait_right(index, half, lower, half_side)
            pl.when(has_up)(lambda: up_copy(index, half, lower).start())
            across_copy(index, half, lower).start()
            mate_copy(index, half, lower, half_side).start()

        @pl.when(upper < LAYERS)
        def _():
            wait_right(index, half, upper, half_side)
            pl.when(has_down)(lambda: down_copy(index, half, upper).start())
            across_copy(index, half, upper).start()
            mate_copy(index, half, upper, half_side).start()

    def chain_finish(index, half):
        leads, follows = (is_helper, is_main) if index else (is_main, is_helper)

        @pl.when(leads)
        def _():
            @pl.loop(0, LAYERS)
            def _(number):
                wait_right(index, half, number, 1 - half_side)
                mate_copy(index, half, number, 1 - half_side).start()

        @pl.when(follows)
        def _():
            @pl.loop(0, LAYERS)
            def _(number):
                wait_right(index, half, number, 0)
                wait_right(index, half, number, 1)

    @pl.when(is_helper)
    def _():
        for half in halves:
            pair_copy(half).start()
        to_diagonal.start()

    @pl.when(is_main)
    def _():
        to_mate.start()
        for half in halves:
            own_piece(half).start()

    left_start(0)

    @pl.when(is_helper)
    def _():
        arrived(piece_slot(1, 0, parity), pair_sem.at[2])
        arrived(piece_slot(1, 0, 1 - parity), pair_sem.at[3])
        chain_send(1, 0)
        for number in range(CHUNKS):
            both_copy(number).start()

    @pl.when(is_main)
    def _():
        for half in halves:
            own_piece(half).wait()
            arrived(piece_slot(0, half, 1 - parity), pair_sem.at[half])
            chain_send(0, half)
        own_tile.start()
        mate_tile.start()

    @pl.loop(0, LAYERS - 1)
    def _(step):
        @pl.when(is_main)
        def _():
            @pl.loop(0, 2)
            def _(turn_half):
                half = jnp.where(turn_half == 0, far_half, 1 - far_half)
                chain_step(0, half, step)

        pl.when(is_helper)(lambda: chain_step(1, 0, step))
        left_hooks(0, step)

        @pl.when(is_main & (step >= 3))
        def _():
            number = step - 3
            arrived(chunk(both, 1 - parity, number), both_sem.at[number])
            mate_both(number).start()


    left_start(1)
    left_finish(0)

    def left_of(index, half):
        return left_high[index, half], left_low[index, half]

    pl.when(is_main)(own_tile.wait)

    @pl.when(is_helper)
    def _():
        arrived(both.at[parity], both_sem.at[CHUNKS])
        for number in range(CHUNKS):
            arrived(chunk(both, 1 - parity, number), both_sem.at[number])

    @pl.loop(0, 3)
    def _(step):
        columns = pl.ds(pl.multiple_of(step * 256, 256), 256)
        total = product(left_of(0, 0), split(both[0, :, columns]))
        total += product(left_of(0, 1), split(both[1, :, columns]))
        mid_high[:, columns], mid_low[:, columns] = split(total)

    def block_ends(half):
        new_row, new_col = moved_to(2 * pair + core), moved_to(2 * target_pair + half)
        index, slot = new_row % 2, new_col % 2
        return block.at[half], fresh.at[index, slot], fresh_sem.at[index, slot]

    def block_copy(half):
        source, target, sem = block_ends(half)
        return remote(source, target, block_out.at[half, 0], sem, block_target(half))

    def relayed_copy(number):
        rows = pl.ds(number * CHUNK, CHUNK)
        return remote(
            block.at[far_half, rows], passing.at[rows], block_out.at[far_half, number],
            passing_sem.at[number], block_target(far_half),
        )

    def passing_copy(number):
        rows = pl.ds(number * CHUNK, CHUNK)
        index, slot = moved_to(relay_old[0]) % 2, moved_to(relay_old[1]) % 2
        return remote(
            passing.at[rows], fresh.at[index, slot, rows], passing_out.at[number],
            fresh_sem.at[index, slot], relay_target,
        )

    @pl.loop(0, 2)
    def _(step):
        half = jnp.where(step == 0, far_half, 1 - far_half)
        chain_finish(0, half)
        turned = right[0, half].reshape(PAIR, ORDER)
        block[half] = product((mid_high[...], mid_low[...]), split(turned))
        here = same(block_target(half))
        through = uses_relay & (half == far_half)

        @pl.when(through)
        def _():
            for number in range(CHUNKS):
                relayed_copy(number).start()

        plain = jnp.logical_not(here) & jnp.logical_not(through)
        pl.when(plain)(lambda: block_copy(half).start())
        pl.when(here)(lambda: pltpu.make_async_copy(*block_ends(half)).start())

    @pl.when(relays)
    def _():
        for number in range(CHUNKS):
            rows = pl.ds(number * CHUNK, CHUNK)
            arrived(passing.at[rows], passing_sem.at[number])
            passing_copy(number).start()

    @pl.loop(0, LAYERS - 1)
    def _(step):
        left_hooks(1, step)

    chain_finish(1, 0)
    left_finish(1)

    def arrive_fresh(index, slot):
        arrived(fresh.at[index, slot], fresh_sem.at[index, slot])

    def mate_fresh(slot):
        ref = fresh.at[core, slot]
        return remote(ref, ref, mate_fresh_out.at[slot], fresh_sem.at[core, slot], mate)

    @pl.loop(0, 2)
    def _(step):
        slot = jnp.where(step == 0, 1 - far_slot, far_slot)
        arrive_fresh(core, slot)
        mate_fresh(slot).start()
        arrive_fresh(1 - core, slot)
        total = product(left_of(1, 0), split(fresh[0, slot]))
        total += product(left_of(1, 1), split(fresh[1, slot]))
        columns = pl.ds(pl.multiple_of(slot * ORDER, 128), ORDER)
        mid_high[:, columns], mid_low[:, columns] = split(total)

    def final_copy(number):
        columns = pl.ds(number * ORDER, ORDER)
        return remote(
            stage.at[:, columns], out.at[:, columns], final_out.at[number], out_sem.at[number],
            diagonal,
        )

    for number in range(2):
        columns = pl.ds(number * ORDER, ORDER)
        turned = right[1, number].reshape(PAIR, ORDER)
        value = product((mid_high[...], mid_low[...]), split(turned))

        @pl.when(is_main)
        def _():
            out[:, columns] = value

        @pl.when(is_helper)
        def _():
            stage[:, columns] = value
            final_copy(number).start()

    for index in range(ROUNDS):
        for half in range(2):
            for reach in range(2):
                device = left_target(half, reach)
                pl.when(jnp.logical_not(same(device)))(left_copy(index, half, reach).wait_send)

        @pl.loop(0, 4)
        def _(number):
            mirror_copy(index, number).wait_send()
            for step in range(1, 4):
                spread_copy(index, 0, number, step).wait_send()
                spread_copy(index, 1, number, step).wait_send()

    for half in range(2):
        through = uses_relay & (half == far_half)
        plain = jnp.logical_not(same(block_target(half))) & jnp.logical_not(through)
        pl.when(plain)(block_copy(half).wait_send)
        mate_fresh(half).wait_send()

    @pl.when(is_helper)
    def _():
        for half in range(2):
            pair_copy(half).wait_send()
        to_diagonal.wait_send()
        for number in range(CHUNKS):
            both_copy(number).wait_send()

    @pl.when(is_main)
    def _():
        mate_tile.wait_send()
        for number in range(CHUNKS):
            mate_both(number).wait_send()

        to_mate.wait_send()

    def chain_left(index, half):
        @pl.loop(0, LAYERS)
        def _(number):
            rises, falls = has_up & (number <= layer), has_down & (number >= layer)
            pl.when(rises)(lambda: up_copy(index, half, number).wait_send())
            pl.when(falls)(lambda: down_copy(index, half, number).wait_send())
            across_copy(index, half, number).wait_send()
            mate_copy(index, half, number, 0).wait_send()
            mate_copy(index, half, number, 1).wait_send()

    pl.when(is_main)(lambda: chain_left(0, 0))
    pl.when(is_main)(lambda: chain_left(0, 1))
    pl.when(is_helper)(lambda: chain_left(1, 0))

    for number in range(CHUNKS):
        pl.when(uses_relay)(relayed_copy(number).wait_send)
        pl.when(relays)(passing_copy(number).wait_send)

    @pl.when(is_helper)
    def _():
        for number in range(2):
            arrived(out.at[:, pl.ds(number * ORDER, ORDER)], out_sem.at[number])
            final_copy(number).wait_send()


def per_device(covariance, rotations, flips):
    shard = rotations[:, 0]
    own_flip = flips[:, lax.axis_index("col")]
    halves = jnp.stack([shard[:, :, :ORDER], shard[:, :, ORDER:]], 1)
    turn = jnp.where((own_flip == 1)[:, None, None, None], halves[:, ::-1], halves)
    dma = pltpu.SemaphoreType.DMA
    return pl.pallas_call(
        kernel,
        out_shape=jax.ShapeDtypeStruct((ORDER, PAIR), jnp.float32),
        in_specs=[pl.BlockSpec(memory_space=pltpu.VMEM)] * 2,
        out_specs=pl.BlockSpec(memory_space=pltpu.VMEM),
        scratch_shapes=[
            pltpu.VMEM((ROUNDS, 2, LAYERS, 2, 2 * PIECE, ORDER), jnp.float32),
            pltpu.VMEM((ROUNDS, SIDES, 2, 4, PIECE, ORDER), jnp.float32),
            pltpu.VMEM((2, ORDER, PAIR), jnp.float32),
            pltpu.VMEM((2, 2, ORDER, ORDER), jnp.float32),
            pltpu.VMEM((2, ORDER, ORDER), jnp.float32),
            pltpu.VMEM((ORDER, PAIR), jnp.float32),
            pltpu.VMEM((ROUNDS, 2, ORDER, ORDER), jnp.bfloat16),
            pltpu.VMEM((ROUNDS, 2, ORDER, ORDER), jnp.bfloat16),
            pltpu.VMEM((ORDER, PAIR), jnp.bfloat16),
            pltpu.VMEM((ORDER, PAIR), jnp.bfloat16),
            pltpu.VMEM((ORDER, ORDER), jnp.float32),
            dma,
            dma((2,)),
            dma((4,)),
            dma((ROUNDS, 2, LAYERS, 2)),
            dma((ROUNDS, 4)),
            dma((ROUNDS, 4)),
            dma((ROUNDS, SIDES, 2)),
            dma((CHUNKS + 1,)),
            dma((2, 2)),
            dma((CHUNKS,)),
            dma((2,)),
            dma((ROUNDS, 2, 2)),
            dma((ROUNDS, 4)),
            dma((ROUNDS, 2, 4, 4)),
            dma((3,)),
            dma((CHUNKS,)),
            dma((ROUNDS, 2, LAYERS, 2)),
            dma((ROUNDS, 2, LAYERS)),
            dma((ROUNDS, 2, LAYERS, 2)),
            dma((CHUNKS + 1,)),
            dma((2, CHUNKS)),
            dma((2,)),
            dma((2,)),
            dma((CHUNKS,)),
        ],
        compiler_params=pltpu.CompilerParams(
            collective_id=0, has_side_effects=True, vmem_limit_bytes=48 * 2**20
        ),
        cost_estimate=pl.CostEstimate(
            flops=12 * ORDER * PAIR * PAIR, bytes_accessed=3 * 2**20, transcendentals=0
        ),
    )(covariance, turn)


def solution(mesh):
    placed = (P("row", "col"), P(None, "col", "row", None), P())
    return jax.shard_map(
        per_device, mesh=mesh, in_specs=placed, out_specs=P("row", "col"), check_vma=False
    )
```

```python
import functools

import jax
import jax.numpy as jnp
from jax import lax
from jax.experimental import pallas as pl
from jax.experimental.pallas import tpu as pltpu
from jax.sharding import PartitionSpec as P

ROUNDS = 2
ORDER = 384
PAIR = 768
LAYERS = 8
SIDES = 4
PIECE = 24
CHUNKS = 4
CHUNK = 96
MESH = pl.DeviceIdType.MESH


def split(value):
    high = value.astype(jnp.bfloat16)
    return high, (value - high.astype(jnp.float32)).astype(jnp.bfloat16)


def product(first, second):
    one = functools.partial(jnp.dot, preferred_element_type=jnp.float32)
    return one(first[0], second[0]) + (one(first[0], second[1]) + one(first[1], second[0]))


def moved_to(place):
    even = jnp.where(place == 0, 0, jnp.where(place == 30, 31, place + 2))
    return jnp.where(place % 2 == 0, even, jnp.where(place == 1, 2, place - 2))


def came_from(place):
    even = jnp.where(place == 0, 0, jnp.where(place == 2, 1, place - 2))
    return jnp.where(place % 2 == 0, even, jnp.where(place == 31, 30, place + 2))


def kernel(
    tile, turn, out, right, left, both, fresh, block, stage, left_high, left_low, mid_high,
    mid_low, passing, tile_sem, own_sem, pair_sem, right_sem, left_sem, mirror_sem, spread_sem, both_sem,
    fresh_sem, passing_sem,
    out_sem, left_out, mirror_out, spread_out, pair_out, both_out, chain_out, across_out,
    mate_out, mate_both_out, block_out, mate_fresh_out, final_out, passing_out,
):
    row, col = lax.axis_index("row"), lax.axis_index("col")
    layer, side = row // SIDES, row % SIDES
    along, far, core = col // 4, (col // 2) % 2, col % 2
    parity, half_side = row % 2, side // 2
    pair, target_pair = row // 2, 2 * (col // 2) + parity
    is_main = core == parity
    is_helper = core != parity
    mate_col = col + 1 - 2 * core
    partner_row = row + 1 - 2 * parity
    across_row = layer * SIDES + (side + 2) % SIDES
    has_down, has_up = layer > 0, layer < LAYERS - 1
    down, up = row - SIDES, row + SIDES
    mate, partner, across = (row, mate_col), (partner_row, col), (across_row, col)
    diagonal = (partner_row, mate_col)

    def same(device):
        return (device[0] == row) & (device[1] == col)

    def left_target(half, reach):
        return (2 * col + layer % 2, 4 * side + 2 * reach + half)

    def left_source(index):
        return (SIDES * (2 * index + parity) + along, pair)

    def peer(step):
        return (row, (col + 4 * step) % 16)

    far_half = jnp.where(target_pair % 2 == 0, 1, 0)
    far_slot = 1 - far_half

    def inside(pair_col):
        return (pair_col != 0) & (pair_col != 15)

    def target_of(old_row, old_col):
        new_row, new_col = moved_to(old_row), moved_to(old_col)
        pair_col = new_col // 2
        return (2 * (new_row // 2) + pair_col % 2, 2 * (pair_col // 2) + new_row % 2)

    def relayed(old_row, pair_col, is_far):
        return is_far & inside(pair_col) & (old_row % 2 == (old_row // 2) % 2)

    def turned_layer(number, half_z):
        wraps = (number < 0) | (number >= LAYERS)
        return (number + LAYERS) % LAYERS, jnp.where(wraps, 1 - half_z, half_z)

    def relay_of(old_row, pair_col):
        odd = (old_row // 2) % 2
        number, half_z = turned_layer(old_row // 4 + 2 * odd - 1, (pair_col // 2) % 2)
        return (
            number * SIDES + 2 * odd + pair_col % 2,
            4 * (pair_col // 4) + 2 * half_z + 1 - pair_col % 2,
        )

    def block_target(half):
        old_row = 2 * pair + core
        end = target_of(old_row, 2 * target_pair + half)
        through = relayed(old_row, target_pair, half == far_half)
        stop = relay_of(old_row, target_pair)
        return tuple(jnp.where(through, one, other) for one, other in zip(stop, end))

    def block_source(slot):
        old_row, old_col = came_from(2 * pair + core), came_from(2 * target_pair + slot)
        pair_col = old_col // 2
        start = (2 * (old_row // 2) + pair_col % 2, 2 * (pair_col // 2) + old_row % 2)
        far = jnp.where(pair_col % 2 == 0, 1, 0)
        through = relayed(old_row, pair_col, old_col % 2 == far)
        stop = relay_of(old_row, pair_col)
        return tuple(jnp.where(through, one, other) for one, other in zip(stop, start))

    relay_layer, relay_far = turned_layer(layer + 1 - 2 * half_side, far)
    relay_pair, relay_col = 2 * relay_layer + half_side, 4 * along + 2 * relay_far + parity
    relays = is_helper & inside(relay_col)
    relay_source = (relay_layer * SIDES + side, 4 * along + 2 * relay_far + half_side)
    own_row = 2 * pair + core
    uses_relay = relayed(own_row, target_pair, jnp.bool_(True))
    relay_old = (2 * relay_pair + half_side, 2 * relay_col + far_half)
    relay_target = target_of(*relay_old)

    barrier = pltpu.get_barrier_semaphore()

    def greet(device, when=None):
        def signal():
            pl.semaphore_signal(barrier, inc=1, device_id=device, device_id_type=MESH)

        if when is None:
            signal()
        else:
            pl.when(when)(signal)

    def count(flag):
        return flag.astype(jnp.int32)

    expected = 6
    for device in (mate, partner, across, peer(1), peer(2), peer(3)):
        greet(device)
    for device, when in (
        (diagonal, is_helper), ((up, col), has_up), ((down, col), has_down)
    ):
        greet(device, when)
        expected += count(when)
    for index in range(SIDES):
        device = left_source(index)
        greet(device, jnp.logical_not(same(device)))
    for half in range(2):
        for reach in range(2):
            expected += 1 - count(same(left_target(half, reach)))
    for slot in range(2):
        device = block_source(slot)
        greet(device, jnp.logical_not(same(device)))
        expected += 1 - count(same(block_target(slot)))
    greet(relay_source, relays)
    expected += count(relays)
    pl.semaphore_wait(barrier, expected)

    def remote(source, target, send_sem, recv_sem, device):
        return pltpu.make_async_remote_copy(
            src_ref=source, dst_ref=target, send_sem=send_sem, recv_sem=recv_sem,
            device_id=device, device_id_type=MESH,
        )

    def arrived(ref, sem):
        remote(ref, ref, sem, sem, partner).wait_recv()

    def left_piece(index, half):
        return turn.at[index, half]

    def left_piece_slot(index):
        return left.at[index, side, layer % 2, layer // 2]

    def left_copy(index, half, reach):
        return remote(
            left_piece(index, half), left_piece_slot(index), left_out.at[index, half, reach],
            left_sem.at[index, layer // 2], left_target(half, reach),
        )

    def left_start(index):
        for half in range(2):
            for reach in range(2):
                here = same(left_target(half, reach))
                pl.when(here)(
                    pltpu.make_async_copy(
                        left_piece(index, half), left_piece_slot(index),
                        left_sem.at[index, layer // 2],
                    ).start
                )
                pl.when(jnp.logical_not(here))(left_copy(index, half, reach).start)

    def mirror_copy(index, number):
        slot = left.at[index, along, parity, number]
        return remote(
            slot, slot, mirror_out.at[index, number], mirror_sem.at[index, number], partner
        )

    def spread_copy(index, which, number, step):
        half = parity if which == 0 else 1 - parity
        slot, sem = left.at[index, along, half, number], spread_sem.at[index, along, half]
        return remote(slot, slot, spread_out.at[index, which, number, step], sem, peer(step))

    def left_pass(index, number):
        arrived(left.at[index, along, parity, number], left_sem.at[index, number])
        mirror_copy(index, number).start()
        for step in range(1, 4):
            spread_copy(index, 0, number, step).start()

    def left_relay(index, number):
        arrived(left.at[index, along, 1 - parity, number], mirror_sem.at[index, number])
        for step in range(1, 4):
            spread_copy(index, 1, number, step).start()

    def left_hooks(index, step):
        pl.when((step >= 1) & (step < 5))(lambda: left_pass(index, step - 1))
        pl.when(step >= 3)(lambda: left_relay(index, step - 3))

    def left_finish(index):
        for step in range(1, 4):
            for which in range(2):
                number = (along + step) % 4
                arrived(left.at[index, number, which], spread_sem.at[index, number, which])
        for half in range(2):
            pieces = [
                left[index, y, z % 2, z // 2]
                for z in range(4 * half, 4 * half + 4) for y in range(SIDES)
            ]
            part = jnp.concatenate(pieces, 0)
            left_high[index, half], left_low[index, half] = split(part.T)

    def slot_of(index, half, number, which):
        return right.at[1, :, number, which] if index else right.at[0, half, number, which]

    def piece_slot(index, half, which):
        rows = pl.ds(pl.multiple_of(PIECE * which, 8), PIECE)
        if index:
            return right.at[1, :, layer, half_side, rows]
        return right.at[0, half, layer, half_side, rows]

    def chunk(ref, index, number):
        return ref.at[index, pl.ds(number * CHUNK, CHUNK)]

    def pair_copy(half):
        return remote(
            turn.at[0, half], piece_slot(0, half, parity), pair_out.at[half], pair_sem.at[half],
            partner,
        )

    def later_copy(device, number):
        return remote(
            turn.at[1], piece_slot(1, 0, parity), pair_out.at[2], pair_sem.at[2 + number], device
        )

    to_mate, to_diagonal = later_copy(mate, 0), later_copy(diagonal, 1)

    def own_piece(half):
        return pltpu.make_async_copy(
            turn.at[0, half], piece_slot(0, half, parity), own_sem.at[half]
        )

    own_tile = pltpu.make_async_copy(tile, both.at[parity], tile_sem)
    mate_tile = remote(tile, both.at[parity], mate_both_out.at[CHUNKS], both_sem.at[CHUNKS], mate)

    def both_copy(number):
        return remote(
            tile.at[pl.ds(number * CHUNK, CHUNK)], chunk(both, parity, number),
            both_out.at[number], both_sem.at[number], partner,
        )

    def mate_both(number):
        slot = chunk(both, 1 - parity, number)
        return remote(slot, slot, mate_both_out.at[number], both_sem.at[number], mate)

    def toward(index, half, number, which, sem, device):
        slot = slot_of(index, half, number, which)
        return remote(slot, slot, sem, right_sem.at[index, half, number, which], device)

    def up_copy(index, half, number):
        return toward(
            index, half, number, half_side, chain_out.at[index, half, number, 0], (up, col)
        )

    def down_copy(index, half, number):
        return toward(
            index, half, number, half_side, chain_out.at[index, half, number, 1], (down, col)
        )

    def across_copy(index, half, number):
        return toward(index, half, number, half_side, across_out.at[index, half, number], across)

    def mate_copy(index, half, number, which):
        return toward(index, half, number, which, mate_out.at[index, half, number, which], mate)

    def wait_right(index, half, number, which):
        arrived(slot_of(index, half, number, which), right_sem.at[index, half, number, which])

    halves = (far_half, 1 - far_half)

    def chain_send(index, half):
        pl.when(has_up)(lambda: up_copy(index, half, layer).start())
        pl.when(has_down)(lambda: down_copy(index, half, layer).start())
        across_copy(index, half, layer).start()
        mate_copy(index, half, layer, half_side).start()

    def chain_step(index, half, step):
        lower, upper = layer - 1 - step, layer + 1 + step

        @pl.when(lower >= 0)
        def _():
            wait_right(index, half, lower, half_side)
            pl.when(has_up)(lambda: up_copy(index, half, lower).start())
            across_copy(index, half, lower).start()
            mate_copy(index, half, lower, half_side).start()

        @pl.when(upper < LAYERS)
        def _():
            wait_right(index, half, upper, half_side)
            pl.when(has_down)(lambda: down_copy(index, half, upper).start())
            across_copy(index, half, upper).start()
            mate_copy(index, half, upper, half_side).start()

    def chain_finish(index, half):
        leads, follows = (is_helper, is_main) if index else (is_main, is_helper)

        @pl.when(leads)
        def _():
            @pl.loop(0, LAYERS)
            def _(number):
                wait_right(index, half, number, 1 - half_side)
                mate_copy(index, half, number, 1 - half_side).start()

        @pl.when(follows)
        def _():
            @pl.loop(0, LAYERS)
            def _(number):
                wait_right(index, half, number, 0)
                wait_right(index, half, number, 1)

    @pl.when(is_helper)
    def _():
        for half in halves:
            pair_copy(half).start()
        to_diagonal.start()

    @pl.when(is_main)
    def _():
        to_mate.start()
        for half in halves:
            own_piece(half).start()

    left_start(0)

    @pl.when(is_helper)
    def _():
        arrived(piece_slot(1, 0, parity), pair_sem.at[2])
        arrived(piece_slot(1, 0, 1 - parity), pair_sem.at[3])
        chain_send(1, 0)
        for number in range(CHUNKS):
            both_copy(number).start()

    @pl.when(is_main)
    def _():
        for half in halves:
            own_piece(half).wait()
            arrived(piece_slot(0, half, 1 - parity), pair_sem.at[half])
            chain_send(0, half)
        own_tile.start()
        mate_tile.start()

    @pl.loop(0, LAYERS - 1)
    def _(step):
        @pl.when(is_main)
        def _():
            @pl.loop(0, 2)
            def _(turn_half):
                half = jnp.where(turn_half == 0, far_half, 1 - far_half)
                chain_step(0, half, step)

        pl.when(is_helper)(lambda: chain_step(1, 0, step))
        left_hooks(0, step)
        pl.when(step == 4)(lambda: left_start(1))

        @pl.when(is_main & (step >= 3))
        def _():
            number = step - 3
            arrived(chunk(both, 1 - parity, number), both_sem.at[number])
            mate_both(number).start()


    left_finish(0)

    def left_of(index, half):
        return left_high[index, half], left_low[index, half]

    pl.when(is_main)(own_tile.wait)

    @pl.when(is_helper)
    def _():
        arrived(both.at[parity], both_sem.at[CHUNKS])
        for number in range(CHUNKS):
            arrived(chunk(both, 1 - parity, number), both_sem.at[number])

    @pl.loop(0, 3)
    def _(step):
        columns = pl.ds(pl.multiple_of(step * 256, 256), 256)
        total = product(left_of(0, 0), split(both[0, :, columns]))
        total += product(left_of(0, 1), split(both[1, :, columns]))
        mid_high[:, columns], mid_low[:, columns] = split(total)

    def block_ends(half):
        new_row, new_col = moved_to(2 * pair + core), moved_to(2 * target_pair + half)
        index, slot = new_row % 2, new_col % 2
        return block.at[half], fresh.at[index, slot], fresh_sem.at[index, slot]

    def block_copy(half):
        source, target, sem = block_ends(half)
        return remote(source, target, block_out.at[half, 0], sem, block_target(half))

    def relayed_copy(number):
        rows = pl.ds(number * CHUNK, CHUNK)
        return remote(
            block.at[far_half, rows], passing.at[rows], block_out.at[far_half, number],
            passing_sem.at[number], block_target(far_half),
        )

    def passing_copy(number):
        rows = pl.ds(number * CHUNK, CHUNK)
        index, slot = moved_to(relay_old[0]) % 2, moved_to(relay_old[1]) % 2
        return remote(
            passing.at[rows], fresh.at[index, slot, rows], passing_out.at[number],
            fresh_sem.at[index, slot], relay_target,
        )

    @pl.loop(0, 2)
    def _(step):
        half = jnp.where(step == 0, far_half, 1 - far_half)
        chain_finish(0, half)
        turned = right[0, half].reshape(PAIR, ORDER)
        block[half] = product((mid_high[...], mid_low[...]), split(turned))
        here = same(block_target(half))
        through = uses_relay & (half == far_half)

        @pl.when(through)
        def _():
            for number in range(CHUNKS):
                relayed_copy(number).start()

        plain = jnp.logical_not(here) & jnp.logical_not(through)
        pl.when(plain)(lambda: block_copy(half).start())
        pl.when(here)(lambda: pltpu.make_async_copy(*block_ends(half)).start())

    @pl.when(relays)
    def _():
        for number in range(CHUNKS):
            rows = pl.ds(number * CHUNK, CHUNK)
            arrived(passing.at[rows], passing_sem.at[number])
            passing_copy(number).start()

    @pl.loop(0, LAYERS - 1)
    def _(step):
        left_hooks(1, step)

    chain_finish(1, 0)
    left_finish(1)

    def arrive_fresh(index, slot):
        arrived(fresh.at[index, slot], fresh_sem.at[index, slot])

    def mate_fresh(slot):
        ref = fresh.at[core, slot]
        return remote(ref, ref, mate_fresh_out.at[slot], fresh_sem.at[core, slot], mate)

    @pl.loop(0, 2)
    def _(step):
        slot = jnp.where(step == 0, 1 - far_slot, far_slot)
        arrive_fresh(core, slot)
        mate_fresh(slot).start()
        arrive_fresh(1 - core, slot)
        total = product(left_of(1, 0), split(fresh[0, slot]))
        total += product(left_of(1, 1), split(fresh[1, slot]))
        columns = pl.ds(pl.multiple_of(slot * ORDER, 128), ORDER)
        mid_high[:, columns], mid_low[:, columns] = split(total)

    def final_copy(number):
        columns = pl.ds(number * ORDER, ORDER)
        return remote(
            stage.at[:, columns], out.at[:, columns], final_out.at[number], out_sem.at[number],
            diagonal,
        )

    for number in range(2):
        columns = pl.ds(number * ORDER, ORDER)
        turned = right[1, number].reshape(PAIR, ORDER)
        value = product((mid_high[...], mid_low[...]), split(turned))

        @pl.when(is_main)
        def _():
            out[:, columns] = value

        @pl.when(is_helper)
        def _():
            stage[:, columns] = value
            final_copy(number).start()

    for index in range(ROUNDS):
        for half in range(2):
            for reach in range(2):
                device = left_target(half, reach)
                pl.when(jnp.logical_not(same(device)))(left_copy(index, half, reach).wait_send)

        @pl.loop(0, 4)
        def _(number):
            mirror_copy(index, number).wait_send()
            for step in range(1, 4):
                spread_copy(index, 0, number, step).wait_send()
                spread_copy(index, 1, number, step).wait_send()

    for half in range(2):
        through = uses_relay & (half == far_half)
        plain = jnp.logical_not(same(block_target(half))) & jnp.logical_not(through)
        pl.when(plain)(block_copy(half).wait_send)
        mate_fresh(half).wait_send()

    @pl.when(is_helper)
    def _():
        for half in range(2):
            pair_copy(half).wait_send()
        to_diagonal.wait_send()
        for number in range(CHUNKS):
            both_copy(number).wait_send()

    @pl.when(is_main)
    def _():
        mate_tile.wait_send()
        for number in range(CHUNKS):
            mate_both(number).wait_send()

        to_mate.wait_send()

    def chain_left(index, half):
        @pl.loop(0, LAYERS)
        def _(number):
            rises, falls = has_up & (number <= layer), has_down & (number >= layer)
            pl.when(rises)(lambda: up_copy(index, half, number).wait_send())
            pl.when(falls)(lambda: down_copy(index, half, number).wait_send())
            across_copy(index, half, number).wait_send()
            mate_copy(index, half, number, 0).wait_send()
            mate_copy(index, half, number, 1).wait_send()

    pl.when(is_main)(lambda: chain_left(0, 0))
    pl.when(is_main)(lambda: chain_left(0, 1))
    pl.when(is_helper)(lambda: chain_left(1, 0))

    for number in range(CHUNKS):
        pl.when(uses_relay)(relayed_copy(number).wait_send)
        pl.when(relays)(passing_copy(number).wait_send)

    @pl.when(is_helper)
    def _():
        for number in range(2):
            arrived(out.at[:, pl.ds(number * ORDER, ORDER)], out_sem.at[number])
            final_copy(number).wait_send()


def per_device(covariance, rotations, flips):
    shard = rotations[:, 0]
    own_flip = flips[:, lax.axis_index("col")]
    halves = jnp.stack([shard[:, :, :ORDER], shard[:, :, ORDER:]], 1)
    turn = jnp.where((own_flip == 1)[:, None, None, None], halves[:, ::-1], halves)
    dma = pltpu.SemaphoreType.DMA
    return pl.pallas_call(
        kernel,
        out_shape=jax.ShapeDtypeStruct((ORDER, PAIR), jnp.float32),
        in_specs=[pl.BlockSpec(memory_space=pltpu.VMEM)] * 2,
        out_specs=pl.BlockSpec(memory_space=pltpu.VMEM),
        scratch_shapes=[
            pltpu.VMEM((ROUNDS, 2, LAYERS, 2, 2 * PIECE, ORDER), jnp.float32),
            pltpu.VMEM((ROUNDS, SIDES, 2, 4, PIECE, ORDER), jnp.float32),
            pltpu.VMEM((2, ORDER, PAIR), jnp.float32),
            pltpu.VMEM((2, 2, ORDER, ORDER), jnp.float32),
            pltpu.VMEM((2, ORDER, ORDER), jnp.float32),
            pltpu.VMEM((ORDER, PAIR), jnp.float32),
            pltpu.VMEM((ROUNDS, 2, ORDER, ORDER), jnp.bfloat16),
            pltpu.VMEM((ROUNDS, 2, ORDER, ORDER), jnp.bfloat16),
            pltpu.VMEM((ORDER, PAIR), jnp.bfloat16),
            pltpu.VMEM((ORDER, PAIR), jnp.bfloat16),
            pltpu.VMEM((ORDER, ORDER), jnp.float32),
            dma,
            dma((2,)),
            dma((4,)),
            dma((ROUNDS, 2, LAYERS, 2)),
            dma((ROUNDS, 4)),
            dma((ROUNDS, 4)),
            dma((ROUNDS, SIDES, 2)),
            dma((CHUNKS + 1,)),
            dma((2, 2)),
            dma((CHUNKS,)),
            dma((2,)),
            dma((ROUNDS, 2, 2)),
            dma((ROUNDS, 4)),
            dma((ROUNDS, 2, 4, 4)),
            dma((3,)),
            dma((CHUNKS,)),
            dma((ROUNDS, 2, LAYERS, 2)),
            dma((ROUNDS, 2, LAYERS)),
            dma((ROUNDS, 2, LAYERS, 2)),
            dma((CHUNKS + 1,)),
            dma((2, CHUNKS)),
            dma((2,)),
            dma((2,)),
            dma((CHUNKS,)),
        ],
        compiler_params=pltpu.CompilerParams(
            collective_id=0, has_side_effects=True, vmem_limit_bytes=48 * 2**20
        ),
        cost_estimate=pl.CostEstimate(
            flops=12 * ORDER * PAIR * PAIR, bytes_accessed=3 * 2**20, transcendentals=0
        ),
    )(covariance, turn)


def solution(mesh):
    placed = (P("row", "col"), P(None, "col", "row", None), P())
    return jax.shard_map(
        per_device, mesh=mesh, in_specs=placed, out_specs=P("row", "col"), check_vma=False
    )
```

```python
import functools

import jax
import jax.numpy as jnp
from jax import lax
from jax.experimental import pallas as pl
from jax.experimental.pallas import tpu as pltpu
from jax.sharding import PartitionSpec as P

ROUNDS = 2
ORDER = 384
PAIR = 768
LAYERS = 8
SIDES = 4
PIECE = 24
CHUNKS = 4
CHUNK = 96
MESH = pl.DeviceIdType.MESH


def split(value):
    high = value.astype(jnp.bfloat16)
    return high, (value - high.astype(jnp.float32)).astype(jnp.bfloat16)


def product(first, second):
    one = functools.partial(jnp.dot, preferred_element_type=jnp.float32)
    return one(first[0], second[0]) + (one(first[0], second[1]) + one(first[1], second[0]))


def moved_to(place):
    even = jnp.where(place == 0, 0, jnp.where(place == 30, 31, place + 2))
    return jnp.where(place % 2 == 0, even, jnp.where(place == 1, 2, place - 2))


def came_from(place):
    even = jnp.where(place == 0, 0, jnp.where(place == 2, 1, place - 2))
    return jnp.where(place % 2 == 0, even, jnp.where(place == 31, 30, place + 2))


def kernel(
    tile, turn, out, right, left, both, fresh, block, stage, left_high, left_low, mid_high,
    mid_low, passing, tile_sem, own_sem, pair_sem, right_sem, left_sem, mirror_sem, spread_sem, both_sem,
    fresh_sem, passing_sem,
    out_sem, left_out, mirror_out, spread_out, pair_out, both_out, chain_out, across_out,
    mate_out, mate_both_out, block_out, mate_fresh_out, final_out, passing_out,
):
    row, col = lax.axis_index("row"), lax.axis_index("col")
    layer, side = row // SIDES, row % SIDES
    along, far, core = col // 4, (col // 2) % 2, col % 2
    parity, half_side = row % 2, side // 2
    pair, target_pair = row // 2, 2 * (col // 2) + parity
    is_main = core == parity
    is_helper = core != parity
    mate_col = col + 1 - 2 * core
    partner_row = row + 1 - 2 * parity
    across_row = layer * SIDES + (side + 2) % SIDES
    has_down, has_up = layer > 0, layer < LAYERS - 1
    down, up = row - SIDES, row + SIDES
    mate, partner, across = (row, mate_col), (partner_row, col), (across_row, col)
    diagonal = (partner_row, mate_col)

    def same(device):
        return (device[0] == row) & (device[1] == col)

    def left_target(half, reach):
        return (2 * col + layer % 2, 4 * side + 2 * reach + half)

    def left_source(index):
        return (SIDES * (2 * index + parity) + along, pair)

    def peer(step):
        return (row, (col + 4 * step) % 16)

    far_half = jnp.where(target_pair % 2 == 0, 1, 0)
    far_slot = 1 - far_half

    def inside(pair_col):
        return (pair_col != 0) & (pair_col != 15)

    def target_of(old_row, old_col):
        new_row, new_col = moved_to(old_row), moved_to(old_col)
        pair_col = new_col // 2
        return (2 * (new_row // 2) + pair_col % 2, 2 * (pair_col // 2) + new_row % 2)

    def relayed(old_row, pair_col, is_far):
        return is_far & inside(pair_col) & (old_row % 2 == (old_row // 2) % 2)

    def turned_layer(number, half_z):
        wraps = (number < 0) | (number >= LAYERS)
        return (number + LAYERS) % LAYERS, jnp.where(wraps, 1 - half_z, half_z)

    def relay_of(old_row, pair_col):
        odd = (old_row // 2) % 2
        number, half_z = turned_layer(old_row // 4 + 2 * odd - 1, (pair_col // 2) % 2)
        return (
            number * SIDES + 2 * odd + pair_col % 2,
            4 * (pair_col // 4) + 2 * half_z + 1 - pair_col % 2,
        )

    def block_target(half):
        old_row = 2 * pair + core
        end = target_of(old_row, 2 * target_pair + half)
        through = relayed(old_row, target_pair, half == far_half)
        stop = relay_of(old_row, target_pair)
        return tuple(jnp.where(through, one, other) for one, other in zip(stop, end))

    def block_source(slot):
        old_row, old_col = came_from(2 * pair + core), came_from(2 * target_pair + slot)
        pair_col = old_col // 2
        start = (2 * (old_row // 2) + pair_col % 2, 2 * (pair_col // 2) + old_row % 2)
        far = jnp.where(pair_col % 2 == 0, 1, 0)
        through = relayed(old_row, pair_col, old_col % 2 == far)
        stop = relay_of(old_row, pair_col)
        return tuple(jnp.where(through, one, other) for one, other in zip(stop, start))

    relay_layer, relay_far = turned_layer(layer + 1 - 2 * half_side, far)
    relay_pair, relay_col = 2 * relay_layer + half_side, 4 * along + 2 * relay_far + parity
    relays = is_helper & inside(relay_col)
    relay_source = (relay_layer * SIDES + side, 4 * along + 2 * relay_far + half_side)
    own_row = 2 * pair + core
    uses_relay = relayed(own_row, target_pair, jnp.bool_(True))
    relay_old = (2 * relay_pair + half_side, 2 * relay_col + far_half)
    relay_target = target_of(*relay_old)

    barrier = pltpu.get_barrier_semaphore()

    def greet(device, when=None):
        def signal():
            pl.semaphore_signal(barrier, inc=1, device_id=device, device_id_type=MESH)

        if when is None:
            signal()
        else:
            pl.when(when)(signal)

    def count(flag):
        return flag.astype(jnp.int32)

    expected = 6
    for device in (mate, partner, across, peer(1), peer(2), peer(3)):
        greet(device)
    for device, when in (
        (diagonal, is_helper), ((up, col), has_up), ((down, col), has_down)
    ):
        greet(device, when)
        expected += count(when)
    for index in range(SIDES):
        device = left_source(index)
        greet(device, jnp.logical_not(same(device)))
    for half in range(2):
        for reach in range(2):
            expected += 1 - count(same(left_target(half, reach)))
    for slot in range(2):
        device = block_source(slot)
        greet(device, jnp.logical_not(same(device)))
        expected += 1 - count(same(block_target(slot)))
    greet(relay_source, relays)
    expected += count(relays)
    pl.semaphore_wait(barrier, expected)

    def remote(source, target, send_sem, recv_sem, device):
        return pltpu.make_async_remote_copy(
            src_ref=source, dst_ref=target, send_sem=send_sem, recv_sem=recv_sem,
            device_id=device, device_id_type=MESH,
        )

    def arrived(ref, sem):
        remote(ref, ref, sem, sem, partner).wait_recv()

    def left_piece(index, half):
        return turn.at[index, half]

    def left_piece_slot(index):
        return left.at[index, side, layer % 2, layer // 2]

    def left_copy(index, half, reach):
        return remote(
            left_piece(index, half), left_piece_slot(index), left_out.at[index, half, reach],
            left_sem.at[index, layer // 2], left_target(half, reach),
        )

    def left_start(index):
        for half in range(2):
            for reach in range(2):
                here = same(left_target(half, reach))
                pl.when(here)(
                    pltpu.make_async_copy(
                        left_piece(index, half), left_piece_slot(index),
                        left_sem.at[index, layer // 2],
                    ).start
                )
                pl.when(jnp.logical_not(here))(left_copy(index, half, reach).start)

    def mirror_copy(index, number):
        slot = left.at[index, along, parity, number]
        return remote(
            slot, slot, mirror_out.at[index, number], mirror_sem.at[index, number], partner
        )

    def spread_copy(index, which, number, step):
        half = parity if which == 0 else 1 - parity
        slot, sem = left.at[index, along, half, number], spread_sem.at[index, along, half]
        return remote(slot, slot, spread_out.at[index, which, number, step], sem, peer(step))

    def left_pass(index, number):
        arrived(left.at[index, along, parity, number], left_sem.at[index, number])
        mirror_copy(index, number).start()
        for step in range(1, 4):
            spread_copy(index, 0, number, step).start()

    def left_relay(index, number):
        arrived(left.at[index, along, 1 - parity, number], mirror_sem.at[index, number])
        for step in range(1, 4):
            spread_copy(index, 1, number, step).start()

    def left_hooks(index, step):
        pl.when((step >= 1) & (step < 5))(lambda: left_pass(index, step - 1))
        pl.when(step >= 3)(lambda: left_relay(index, step - 3))

    def left_finish(index):
        for step in range(1, 4):
            for which in range(2):
                number = (along + step) % 4
                arrived(left.at[index, number, which], spread_sem.at[index, number, which])
        for half in range(2):
            pieces = [
                left[index, y, z % 2, z // 2]
                for z in range(4 * half, 4 * half + 4) for y in range(SIDES)
            ]
            part = jnp.concatenate(pieces, 0)
            left_high[index, half], left_low[index, half] = split(part.T)

    def slot_of(index, half, number, which):
        return right.at[1, :, number, which] if index else right.at[0, half, number, which]

    def piece_slot(index, half, which):
        rows = pl.ds(pl.multiple_of(PIECE * which, 8), PIECE)
        if index:
            return right.at[1, :, layer, half_side, rows]
        return right.at[0, half, layer, half_side, rows]

    def chunk(ref, index, number):
        return ref.at[index, pl.ds(number * CHUNK, CHUNK)]

    def pair_copy(half):
        return remote(
            turn.at[0, half], piece_slot(0, half, parity), pair_out.at[half], pair_sem.at[half],
            partner,
        )

    def later_copy(device, number):
        return remote(
            turn.at[1], piece_slot(1, 0, parity), pair_out.at[2], pair_sem.at[2 + number], device
        )

    to_mate, to_diagonal = later_copy(mate, 0), later_copy(diagonal, 1)

    def own_piece(half):
        return pltpu.make_async_copy(
            turn.at[0, half], piece_slot(0, half, parity), own_sem.at[half]
        )

    own_tile = pltpu.make_async_copy(tile, both.at[parity], tile_sem)
    mate_tile = remote(tile, both.at[parity], mate_both_out.at[CHUNKS], both_sem.at[CHUNKS], mate)

    def both_copy(number):
        return remote(
            tile.at[pl.ds(number * CHUNK, CHUNK)], chunk(both, parity, number),
            both_out.at[number], both_sem.at[number], partner,
        )

    def mate_both(number):
        slot = chunk(both, 1 - parity, number)
        return remote(slot, slot, mate_both_out.at[number], both_sem.at[number], mate)

    def toward(index, half, number, which, sem, device):
        slot = slot_of(index, half, number, which)
        return remote(slot, slot, sem, right_sem.at[index, half, number, which], device)

    def up_copy(index, half, number):
        return toward(
            index, half, number, half_side, chain_out.at[index, half, number, 0], (up, col)
        )

    def down_copy(index, half, number):
        return toward(
            index, half, number, half_side, chain_out.at[index, half, number, 1], (down, col)
        )

    def across_copy(index, half, number):
        return toward(index, half, number, half_side, across_out.at[index, half, number], across)

    def mate_copy(index, half, number, which):
        return toward(index, half, number, which, mate_out.at[index, half, number, which], mate)

    def wait_right(index, half, number, which):
        arrived(slot_of(index, half, number, which), right_sem.at[index, half, number, which])

    halves = (far_half, 1 - far_half)

    def chain_send(index, half):
        pl.when(has_up)(lambda: up_copy(index, half, layer).start())
        pl.when(has_down)(lambda: down_copy(index, half, layer).start())
        across_copy(index, half, layer).start()
        mate_copy(index, half, layer, half_side).start()

    def chain_step(index, half, step):
        lower, upper = layer - 1 - step, layer + 1 + step

        @pl.when(lower >= 0)
        def _():
            wait_right(index, half, lower, half_side)
            pl.when(has_up)(lambda: up_copy(index, half, lower).start())
            across_copy(index, half, lower).start()
            mate_copy(index, half, lower, half_side).start()

        @pl.when(upper < LAYERS)
        def _():
            wait_right(index, half, upper, half_side)
            pl.when(has_down)(lambda: down_copy(index, half, upper).start())
            across_copy(index, half, upper).start()
            mate_copy(index, half, upper, half_side).start()

    def chain_finish(index, half):
        leads, follows = (is_helper, is_main) if index else (is_main, is_helper)

        @pl.when(leads)
        def _():
            @pl.loop(0, LAYERS)
            def _(number):
                wait_right(index, half, number, 1 - half_side)
                mate_copy(index, half, number, 1 - half_side).start()

        @pl.when(follows)
        def _():
            @pl.loop(0, LAYERS)
            def _(number):
                wait_right(index, half, number, 0)
                wait_right(index, half, number, 1)

    @pl.when(is_helper)
    def _():
        for half in halves:
            pair_copy(half).start()
        to_diagonal.start()

    @pl.when(is_main)
    def _():
        to_mate.start()
        for half in halves:
            own_piece(half).start()

    left_start(0)

    @pl.when(is_helper)
    def _():
        arrived(piece_slot(1, 0, parity), pair_sem.at[2])
        arrived(piece_slot(1, 0, 1 - parity), pair_sem.at[3])
        chain_send(1, 0)
        for number in range(CHUNKS):
            both_copy(number).start()

    @pl.when(is_main)
    def _():
        for half in halves:
            own_piece(half).wait()
            arrived(piece_slot(0, half, 1 - parity), pair_sem.at[half])
            chain_send(0, half)
        own_tile.start()
        mate_tile.start()

    @pl.loop(0, LAYERS - 1)
    def _(step):
        @pl.when(is_main)
        def _():
            @pl.loop(0, 2)
            def _(turn_half):
                half = jnp.where(turn_half == 0, far_half, 1 - far_half)
                chain_step(0, half, step)

        pl.when(is_helper)(lambda: chain_step(1, 0, step))
        left_hooks(0, step)

        @pl.when(is_main & (step >= 3))
        def _():
            number = step - 3
            arrived(chunk(both, 1 - parity, number), both_sem.at[number])
            mate_both(number).start()


    left_start(1)
    left_finish(0)

    def left_of(index, half):
        return left_high[index, half], left_low[index, half]

    pl.when(is_main)(own_tile.wait)

    @pl.when(is_helper)
    def _():
        arrived(both.at[parity], both_sem.at[CHUNKS])
        for number in range(CHUNKS):
            arrived(chunk(both, 1 - parity, number), both_sem.at[number])

    @pl.loop(0, 3)
    def _(step):
        columns = pl.ds(pl.multiple_of(step * 256, 256), 256)
        total = product(left_of(0, 0), split(both[0, :, columns]))
        total += product(left_of(0, 1), split(both[1, :, columns]))
        mid_high[:, columns], mid_low[:, columns] = split(total)

    def block_ends(half):
        new_row, new_col = moved_to(2 * pair + core), moved_to(2 * target_pair + half)
        index, slot = new_row % 2, new_col % 2
        return block.at[half], fresh.at[index, slot], fresh_sem.at[index, slot]

    def block_copy(half):
        source, target, sem = block_ends(half)
        return remote(source, target, block_out.at[half, 0], sem, block_target(half))

    def relayed_copy(number):
        rows = pl.ds(number * CHUNK, CHUNK)
        return remote(
            block.at[far_half, rows], passing.at[rows], block_out.at[far_half, number],
            passing_sem.at[number], block_target(far_half),
        )

    def passing_copy(number):
        rows = pl.ds(number * CHUNK, CHUNK)
        index, slot = moved_to(relay_old[0]) % 2, moved_to(relay_old[1]) % 2
        return remote(
            passing.at[rows], fresh.at[index, slot, rows], passing_out.at[number],
            fresh_sem.at[index, slot], relay_target,
        )

    @pl.loop(0, 2)
    def _(step):
        half = jnp.where(step == 0, far_half, 1 - far_half)
        chain_finish(0, half)
        turned = right[0, half].reshape(PAIR, ORDER)
        block[half] = product((mid_high[...], mid_low[...]), split(turned))
        here = same(block_target(half))
        through = uses_relay & (half == far_half)

        @pl.when(through)
        def _():
            for number in range(CHUNKS):
                relayed_copy(number).start()

        plain = jnp.logical_not(here) & jnp.logical_not(through)
        pl.when(plain)(lambda: block_copy(half).start())
        pl.when(here)(lambda: pltpu.make_async_copy(*block_ends(half)).start())

    @pl.when(relays)
    def _():
        for number in range(CHUNKS):
            rows = pl.ds(number * CHUNK, CHUNK)
            arrived(passing.at[rows], passing_sem.at[number])
            passing_copy(number).start()

    @pl.loop(0, LAYERS - 1)
    def _(step):
        left_hooks(1, step)

    chain_finish(1, 0)
    left_finish(1)

    def arrive_fresh(index, slot):
        arrived(fresh.at[index, slot], fresh_sem.at[index, slot])

    def mate_fresh(slot):
        ref = fresh.at[core, slot]
        return remote(ref, ref, mate_fresh_out.at[slot], fresh_sem.at[core, slot], mate)

    def rows_of(number, slot):
        return right[1, number, pl.ds(4 * slot, 4)].reshape(ORDER, ORDER)

    def second_left(slot):
        arrive_fresh(core, slot)
        mate_fresh(slot).start()
        total = product(left_of(1, core), split(fresh[core, slot]))
        arrive_fresh(1 - core, slot)
        return split(total + product(left_of(1, 1 - core), split(fresh[1 - core, slot])))

    near = second_left(1 - far_slot)
    for number in range(2):
        stage[:, pl.ds(number * ORDER, ORDER)] = product(near, split(rows_of(number, 1 - far_slot)))
    mid_high[:, :ORDER], mid_low[:, :ORDER] = second_left(far_slot)

    def final_copy(number):
        columns = pl.ds(number * ORDER, ORDER)
        return remote(
            stage.at[:, columns], out.at[:, columns], final_out.at[number], out_sem.at[number],
            diagonal,
        )

    for number in range(2):
        columns = pl.ds(number * ORDER, ORDER)
        ahead = (mid_high[:, :ORDER], mid_low[:, :ORDER])
        value = stage[:, columns] + product(ahead, split(rows_of(number, far_slot)))

        @pl.when(is_main)
        def _():
            out[:, columns] = value

        @pl.when(is_helper)
        def _():
            stage[:, columns] = value
            final_copy(number).start()

    for index in range(ROUNDS):
        for half in range(2):
            for reach in range(2):
                device = left_target(half, reach)
                pl.when(jnp.logical_not(same(device)))(left_copy(index, half, reach).wait_send)

        @pl.loop(0, 4)
        def _(number):
            mirror_copy(index, number).wait_send()
            for step in range(1, 4):
                spread_copy(index, 0, number, step).wait_send()
                spread_copy(index, 1, number, step).wait_send()

    for half in range(2):
        through = uses_relay & (half == far_half)
        plain = jnp.logical_not(same(block_target(half))) & jnp.logical_not(through)
        pl.when(plain)(block_copy(half).wait_send)
        mate_fresh(half).wait_send()

    @pl.when(is_helper)
    def _():
        for half in range(2):
            pair_copy(half).wait_send()
        to_diagonal.wait_send()
        for number in range(CHUNKS):
            both_copy(number).wait_send()

    @pl.when(is_main)
    def _():
        mate_tile.wait_send()
        for number in range(CHUNKS):
            mate_both(number).wait_send()

        to_mate.wait_send()

    def chain_left(index, half):
        @pl.loop(0, LAYERS)
        def _(number):
            rises, falls = has_up & (number <= layer), has_down & (number >= layer)
            pl.when(rises)(lambda: up_copy(index, half, number).wait_send())
            pl.when(falls)(lambda: down_copy(index, half, number).wait_send())
            across_copy(index, half, number).wait_send()
            mate_copy(index, half, number, 0).wait_send()
            mate_copy(index, half, number, 1).wait_send()

    pl.when(is_main)(lambda: chain_left(0, 0))
    pl.when(is_main)(lambda: chain_left(0, 1))
    pl.when(is_helper)(lambda: chain_left(1, 0))

    for number in range(CHUNKS):
        pl.when(uses_relay)(relayed_copy(number).wait_send)
        pl.when(relays)(passing_copy(number).wait_send)

    @pl.when(is_helper)
    def _():
        for number in range(2):
            arrived(out.at[:, pl.ds(number * ORDER, ORDER)], out_sem.at[number])
            final_copy(number).wait_send()


def per_device(covariance, rotations, flips):
    shard = rotations[:, 0]
    own_flip = flips[:, lax.axis_index("col")]
    halves = jnp.stack([shard[:, :, :ORDER], shard[:, :, ORDER:]], 1)
    turn = jnp.where((own_flip == 1)[:, None, None, None], halves[:, ::-1], halves)
    dma = pltpu.SemaphoreType.DMA
    return pl.pallas_call(
        kernel,
        out_shape=jax.ShapeDtypeStruct((ORDER, PAIR), jnp.float32),
        in_specs=[pl.BlockSpec(memory_space=pltpu.VMEM)] * 2,
        out_specs=pl.BlockSpec(memory_space=pltpu.VMEM),
        scratch_shapes=[
            pltpu.VMEM((ROUNDS, 2, LAYERS, 2, 2 * PIECE, ORDER), jnp.float32),
            pltpu.VMEM((ROUNDS, SIDES, 2, 4, PIECE, ORDER), jnp.float32),
            pltpu.VMEM((2, ORDER, PAIR), jnp.float32),
            pltpu.VMEM((2, 2, ORDER, ORDER), jnp.float32),
            pltpu.VMEM((2, ORDER, ORDER), jnp.float32),
            pltpu.VMEM((ORDER, PAIR), jnp.float32),
            pltpu.VMEM((ROUNDS, 2, ORDER, ORDER), jnp.bfloat16),
            pltpu.VMEM((ROUNDS, 2, ORDER, ORDER), jnp.bfloat16),
            pltpu.VMEM((ORDER, PAIR), jnp.bfloat16),
            pltpu.VMEM((ORDER, PAIR), jnp.bfloat16),
            pltpu.VMEM((ORDER, ORDER), jnp.float32),
            dma,
            dma((2,)),
            dma((4,)),
            dma((ROUNDS, 2, LAYERS, 2)),
            dma((ROUNDS, 4)),
            dma((ROUNDS, 4)),
            dma((ROUNDS, SIDES, 2)),
            dma((CHUNKS + 1,)),
            dma((2, 2)),
            dma((CHUNKS,)),
            dma((2,)),
            dma((ROUNDS, 2, 2)),
            dma((ROUNDS, 4)),
            dma((ROUNDS, 2, 4, 4)),
            dma((3,)),
            dma((CHUNKS,)),
            dma((ROUNDS, 2, LAYERS, 2)),
            dma((ROUNDS, 2, LAYERS)),
            dma((ROUNDS, 2, LAYERS, 2)),
            dma((CHUNKS + 1,)),
            dma((2, CHUNKS)),
            dma((2,)),
            dma((2,)),
            dma((CHUNKS,)),
        ],
        compiler_params=pltpu.CompilerParams(
            collective_id=0, has_side_effects=True, vmem_limit_bytes=48 * 2**20
        ),
        cost_estimate=pl.CostEstimate(
            flops=12 * ORDER * PAIR * PAIR, bytes_accessed=3 * 2**20, transcendentals=0
        ),
    )(covariance, turn)


def solution(mesh):
    placed = (P("row", "col"), P(None, "col", "row", None), P())
    return jax.shard_map(
        per_device, mesh=mesh, in_specs=placed, out_specs=P("row", "col"), check_vma=False
    )
```
